256 devices in a mesh: mp: 4 (over y), nodes: 64 (over z, x, core).
Axes of the slice: x: 4, y: 4, z: 8, core: 2. Of those that a mesh axis runs over, the one named last changes fastest.
Arguments:
- grid_latent: float32 [131072, 512], P('nodes'), may hold values from -6 to 6
- mesh_latent: float32 [8192, 512], P('nodes'), may hold values from -250 to 250
- enc_grid_w: float32 [512, 512], P(None, 'mp'), may hold values from -0.25 to 0.25
- enc_mesh_w: float32 [512, 512], P(None, 'mp'), may hold values from -0.25 to 0.25
- enc_out_w: float32 [512, 512], P('mp'), may hold values from -0.25 to 0.25
- block_gain: float32 [512], replicated, may hold values from 0.5 to 1.5
- query_w: float32 [512, 512], P(None, 'mp'), may hold values from -1 to 1
- key_w: float32 [512, 512], P(None, 'mp'), may hold values from -1 to 1
- value_w: float32 [512, 512], P(None, 'mp'), may hold values from -0.25 to 0.25
- out_w: float32 [512, 512], P('mp'), may hold values from -0.25 to 0.25
- up_w: float32 [512, 2048], P(None, 'mp'), may hold values from -0.25 to 0.25
- down_w: float32 [2048, 512], P('mp'), may hold values from -0.125 to 0.125
- dec_gain: float32 [512], replicated, may hold values from 0.5 to 1.5
- dec_grid_w: float32 [512, 512], P(None, 'mp'), may hold values from -0.25 to 0.25
- dec_mesh_w: float32 [512, 512], P(None, 'mp'), may hold values from -0.25 to 0.25
- dec_out_w: float32 [512, 512], P('mp'), may hold values from -0.25 to 0.25
- neighbor_blocks: int32 [64, 16], replicated, may hold values from 0 to 63, as said below
- enc_tiles: int32 [2048, 2], P('nodes'), may hold values from -1 to 1023, as said below
- enc_edges: int32 [2048, 2, 128], P('nodes'), may hold values from 0 to 127
- dec_tiles: int32 [3072, 2], P('nodes'), may hold values from 0 to 1023, as said below
- dec_edges: int32 [3072, 2, 128], P('nodes'), may hold values from 0 to 127
Outputs:
- grid_out: float32 [131072, 512], P('nodes', 'mp')
The draws below stay inside these ranges and needn't reach their ends.
Inputs may be any that keep to these rules, and one draw needn't show every extreme that they name: `neighbor_blocks`: rows i * 1 to (i + 1) - 1 are the query blocks of index i of nodes; among all entries of those rows, the blocks of any one index j of nodes (ids j * 1 to (j + 1) - 1) are named at most 1 times, and for every i some j is named exactly 1 times. Entries may repeat. `enc_tiles`: tile slots i * 32 to (i + 1) * 32 - 1 belong to index i of nodes; a live tile names a grid block and a mesh block both of index i; an unused slot holds -1 in both columns; on each index the live slots come first, their number differs between indices, and some index has all 32 slots live. `dec_tiles`: tiles i * 48 to (i + 1) * 48 - 1 belong to index i of nodes; each names a grid block of index i and a mesh block of index i - 1, i or i + 1 of nodes (counted around the axis).
All inputs are finite; a program needn't handle non-finite values.
Results may differ from the reference program's by a relative error of at most 0.000098.
Values sent between devices are 32-bit elements; how exact they have to be, the bound alone decides.
A program may use at most 128 MiB of HBM per device.

```python
import math
import jax
import jax.numpy as jnp
from jax import lax

D = 512
HEADS = 4
HEAD_DIM = 128
FF = 2048
EDGE_HIDDEN = 512
NODE_BLOCK = 128
NBR = 16
GRID_DEV = 2048
BPD = 1
GRID = 131072
MBLOCKS = 64
MESH = 8192
ET_DEV = 32
DT_DEV = 48
ETILES = 2048
DTILES = 3072


def drawn_weight(key, salt):
    entries = jax.random.normal(jax.random.fold_in(key, salt), (D, D), jnp.float32)
    return jnp.clip(entries, -4.0, 4.0) / math.sqrt(D)


def draw_query_w(key, part):
    weight_rows = drawn_weight(key, 61)
    return weight_rows


def draw_key_w(key, part):
    weight_rows = drawn_weight(key, 62)
    return weight_rows


def draw_mesh_latent(key, part):
    latent = jnp.clip(jax.random.normal(jax.random.fold_in(key, 71), (MESH, D), jnp.float32), -6.0, 6.0)
    return latent


def draw_neighbor_blocks(key, part):
    devices = MBLOCKS // BPD
    request_count = BPD * NBR
    slot_count = max(1, 2 * request_count // devices)

    def one_device(device_key):
        first, second, third = jax.random.split(device_key, 3)
        order = jax.random.permutation(first, devices)
        owners = order[jnp.arange(request_count) // slot_count]
        within_owner = jax.random.randint(second, (request_count,), 0, BPD)
        mixing = jax.random.permutation(third, request_count)
        return (owners * BPD + within_owner)[mixing]
    device_keys = jax.random.split(jax.random.fold_in(key, 11), devices)
    listed = jax.vmap(one_device)(device_keys)
    return listed.reshape(MBLOCKS, NBR).astype(jnp.int32)


def draw_enc_tiles(key, part):
    devices = MBLOCKS // BPD
    per_device = ET_DEV
    grid_blocks = GRID_DEV // NODE_BLOCK
    first, second, third, fourth = jax.random.split(jax.random.fold_in(key, 23), 4)
    raw_count = jax.random.randint(first, (devices,), 0, per_device)
    used = 1 + raw_count * raw_count // per_device
    busiest = jax.random.randint(second, (), 0, devices)
    used = jnp.where(jnp.arange(devices) == busiest, per_device, used)
    tile_live = jnp.arange(per_device)[None, :] < used[:, None]
    device = jnp.arange(devices)[:, None]
    source = device * grid_blocks + jax.random.randint(third, (devices, per_device), 0, grid_blocks)
    target = device * BPD + jax.random.randint(fourth, (devices, per_device), 0, BPD)
    tile_ids = jnp.stack([jnp.where(tile_live, source, -1), jnp.where(tile_live, target, -1)], axis=-1)
    return tile_ids.reshape(devices * per_device, 2).astype(jnp.int32)


def draw_dec_tiles(key, part):
    devices = MBLOCKS // BPD
    per_device = DT_DEV
    grid_blocks = GRID_DEV // NODE_BLOCK
    first, second, third = jax.random.split(jax.random.fold_in(key, 37), 3)
    device = jnp.arange(devices)[:, None]
    beside = jax.random.randint(first, (devices, per_device), -1, 2)
    source = (device + beside) % devices * BPD + jax.random.randint(second, (devices, per_device), 0, BPD)
    target = device * grid_blocks + jax.random.randint(third, (devices, per_device), 0, grid_blocks)
    tile_ids = jnp.stack([source, target], axis=-1)
    return tile_ids.reshape(devices * per_device, 2).astype(jnp.int32)


def with_ends(values, stream_key, least, high):
    shape = values.shape
    index_at = [jax.random.randint(jax.random.fold_in(stream_key, axis), (), 0, shape[axis]) for axis in range(len(shape))]
    values = values.at[tuple(index_at)].set(least)
    longest = shape.index(max(shape))
    index_at[longest] = (index_at[longest] + 1) % shape[longest]
    return values.at[tuple(index_at)].set(high)


def block_scale(own_key, dims, pieces, low, largest):
    factor_of = 1.0
    for position, blocks in pieces:
        steps = jax.random.uniform(jax.random.fold_in(jax.random.fold_in(own_key, 6), position), (blocks,), jnp.float32, low / len(pieces), largest / len(pieces))
        factor_of = factor_of * jnp.repeat(jnp.exp(steps), dims[position] // blocks).reshape((-1,) + (1,) * (len(dims) - 1 - position))
    return factor_of


def centred(stream_key, dims, scale, most, shards=(), dtype=jnp.bfloat16):
    level = block_scale(stream_key, dims, shards, -0.22, 0.18) if shards else 1.0
    values = jax.random.normal(stream_key, dims, jnp.float32) * scale * level
    return jnp.minimum(jnp.maximum(values, -most), most).astype(dtype)


def setup_inputs(seed: int = 0) -> dict:
    arg_keys = jax.random.split(jax.random.key(seed), 22)
    return {
        "grid_latent": centred(arg_keys[0], (GRID, D), 1.0, 6.0, ((0, 64),), jnp.float32),
        "mesh_latent": draw_mesh_latent(jax.random.fold_in(arg_keys[21], 71), 0),
        "enc_grid_w": centred(arg_keys[2], (D, EDGE_HIDDEN), D ** -0.5, 0.25, ((1, 4),), jnp.float32),
        "enc_mesh_w": centred(arg_keys[3], (D, EDGE_HIDDEN), D ** -0.5, 0.25, ((1, 4),), jnp.float32),
        "enc_out_w": centred(arg_keys[4], (EDGE_HIDDEN, D), EDGE_HIDDEN ** -0.5, 0.25, ((0, 4),), jnp.float32),
        "block_gain": jnp.clip(1.0 + 0.1 * jax.random.normal(arg_keys[5], (D,), jnp.float32), 0.5, 1.5),
        "query_w": draw_query_w(jax.random.fold_in(arg_keys[21], 71), 0),
        "key_w": draw_key_w(jax.random.fold_in(arg_keys[21], 71), 0),
        "value_w": centred(arg_keys[8], (D, D), D ** -0.5, 0.25, ((1, 4),), jnp.float32),
        "out_w": centred(arg_keys[9], (D, D), D ** -0.5, 0.25, ((0, 4),), jnp.float32),
        "up_w": centred(arg_keys[10], (D, FF), D ** -0.5, 0.25, ((1, 4),), jnp.float32),
        "down_w": centred(arg_keys[11], (FF, D), FF ** -0.5, 0.125, ((0, 4),), jnp.float32),
        "dec_gain": jnp.clip(1.0 + 0.1 * jax.random.normal(arg_keys[12], (D,), jnp.float32), 0.5, 1.5),
        "dec_grid_w": centred(arg_keys[13], (D, EDGE_HIDDEN), D ** -0.5, 0.25, ((1, 4),), jnp.float32),
        "dec_mesh_w": centred(arg_keys[14], (D, EDGE_HIDDEN), D ** -0.5, 0.25, ((1, 4),), jnp.float32),
        "dec_out_w": centred(arg_keys[15], (EDGE_HIDDEN, D), EDGE_HIDDEN ** -0.5, 0.25, ((0, 4),), jnp.float32),
        "neighbor_blocks": draw_neighbor_blocks(jax.random.fold_in(arg_keys[21], 71), 0),
        "enc_tiles": draw_enc_tiles(jax.random.fold_in(arg_keys[21], 71), 0),
        "enc_edges": with_ends(jax.random.randint(arg_keys[18], (ETILES, 2, NODE_BLOCK), 0, NODE_BLOCK), jax.random.fold_in(arg_keys[18], 1), 0, NODE_BLOCK - 1).astype(jnp.int32),
        "dec_tiles": draw_dec_tiles(jax.random.fold_in(arg_keys[21], 71), 0),
        "dec_edges": with_ends(jax.random.randint(arg_keys[20], (DTILES, 2, NODE_BLOCK), 0, NODE_BLOCK), jax.random.fold_in(arg_keys[20], 1), 0, NODE_BLOCK - 1).astype(jnp.int32),
    }


FULL_PRECISION = lax.Precision.HIGHEST

def product(matrix, weight):
    return jnp.dot(matrix, weight, precision=FULL_PRECISION, preferred_element_type=jnp.float32)

def layer_norm(inputs, scales):
    centre = lax.optimization_barrier(jnp.mean(inputs, axis=-1, keepdims=True))
    shifted = inputs - centre
    spread = lax.optimization_barrier(jnp.mean(shifted * shifted, axis=-1, keepdims=True))
    return shifted * lax.rsqrt(spread + 1e-05) * scales

def edge_pass(source_side, target_side, tile_ids, edge_ids, targets):
    tile_live = tile_ids[:, 0] >= 0
    source = jnp.where(tile_live, tile_ids[:, 0], 0)[:, None] * NODE_BLOCK + edge_ids[:, 0, :]
    target = jnp.where(tile_live, tile_ids[:, 1], 0)[:, None] * NODE_BLOCK + edge_ids[:, 1, :]
    message = jax.nn.silu(source_side[source] + target_side[target])
    message = message * tile_live[:, None, None].astype(jnp.float32)
    hidden_cols = message.shape[-1]
    return jax.ops.segment_sum(message.reshape(-1, hidden_cols), target.reshape(-1), num_segments=targets)

def attention(queries, key_rows, value_rows, neighbor_blocks):
    blocks = queries.shape[0] // NODE_BLOCK
    query_blocks = queries.reshape(blocks, NODE_BLOCK, HEADS, HEAD_DIM)
    key_blocks = key_rows.reshape(blocks, NODE_BLOCK, HEADS, HEAD_DIM)
    value_blocks = value_rows.reshape(blocks, NODE_BLOCK, HEADS, HEAD_DIM)

    def one_block(inputs):
        block_queries, listed = inputs
        near_keys = key_blocks[listed].reshape(-1, HEADS, HEAD_DIM)
        near_values = value_blocks[listed].reshape(-1, HEADS, HEAD_DIM)
        scores = jnp.einsum('qhd,khd->hqk', block_queries, near_keys, precision=FULL_PRECISION) / math.sqrt(HEAD_DIM)
        weights = jax.nn.softmax(scores, axis=-1)
        return jnp.einsum('hqk,khd->qhd', weights, near_values, precision=FULL_PRECISION)
    attended = lax.map(one_block, (query_blocks, neighbor_blocks))
    return attended.reshape(-1, HEADS * HEAD_DIM)

def reference(grid_latent, mesh_latent, enc_grid_w, enc_mesh_w, enc_out_w, block_gain, query_w, key_w, value_w, out_w, up_w, down_w, dec_gain, dec_grid_w, dec_mesh_w, dec_out_w, neighbor_blocks, enc_tiles, enc_edges, dec_tiles, dec_edges):
    grid_enc = product(grid_latent, enc_grid_w)
    mesh_enc = product(mesh_latent, enc_mesh_w)
    enc_agg = edge_pass(grid_enc, mesh_enc, enc_tiles, enc_edges, mesh_latent.shape[0])
    mesh_one = mesh_latent + product(enc_agg, enc_out_w)
    normed = layer_norm(mesh_one, block_gain)
    queries = product(normed, query_w)
    key_rows = product(normed, key_w)
    value_rows = product(normed, value_w)
    attended = attention(queries, key_rows, value_rows, neighbor_blocks)
    hidden = jax.nn.silu(product(normed, up_w))
    mesh_two = mesh_one + product(attended, out_w) + product(hidden, down_w)
    mesh_dec = product(layer_norm(mesh_two, dec_gain), dec_mesh_w)
    grid_dec = product(grid_latent, dec_grid_w)
    dec_agg = edge_pass(mesh_dec, grid_dec, dec_tiles, dec_edges, grid_latent.shape[0])
    return grid_latent + product(dec_agg, dec_out_w)
```

```python
import functools
import math

import jax
import jax.numpy as jnp
from jax import lax
from jax.experimental import pallas as pl
from jax.experimental.pallas import tpu as pltpu
from jax.sharding import PartitionSpec as P

HEAD_DIM = 128
BLOCK = 128
FULL = lax.Precision.HIGHEST
F32 = jnp.float32
BF16 = jnp.bfloat16


def product(matrix, weight):
    return jnp.dot(matrix, weight, precision=FULL, preferred_element_type=F32)


def layer_norm(inputs, scales):
    centre = jnp.mean(inputs, axis=-1, keepdims=True)
    shifted = inputs - centre
    spread = jnp.mean(shifted * shifted, axis=-1, keepdims=True)
    return shifted * lax.rsqrt(spread + 1e-05) * scales


def split(x):
    high = x.astype(BF16)
    low = (x - high.astype(F32)).astype(BF16)
    return high, low


def mm(a, b):
    return jnp.dot(a, b, preferred_element_type=F32)


def silu(v):
    return v * (1.0 / (1.0 + jnp.exp(-v)))


def as_column(row):
    return jnp.broadcast_to(row, (8, BLOCK)).T[:, 0:1]


def one_hot_rows(row):
    lane = lax.broadcasted_iota(jnp.int32, (BLOCK, BLOCK), 1)
    return jnp.where(as_column(row) == lane, 1.0, 0.0).astype(BF16)


def one_hot_cols(row):
    sub = lax.broadcasted_iota(jnp.int32, (BLOCK, BLOCK), 0)
    return jnp.where(row == sub, 1.0, 0.0).astype(BF16)


def encoder_kernel(
    tiles, grid_ref, wg_ref, mesh_ref, wm_ref, edges_ref, out_ref, wcat, gcat, mcat, acc
):
    step = pl.program_id(0)
    steps = pl.num_programs(0)
    rows, hid = grid_ref.shape[0], wg_ref.shape[1]
    blocks = gcat.shape[0] // BLOCK
    slots = edges_ref.shape[0]

    @pl.when(step == 0)
    def _():
        high, low = split(wg_ref[...])
        wcat[:, :hid] = high
        wcat[:, hid:] = low
        mesh_enc = product(mesh_ref[...], wm_ref[...])
        high, low = split(mesh_enc)
        mcat[:, :hid] = high
        mcat[:, hid:] = low
        acc[...] = jnp.zeros_like(acc)

    xh, xl = split(grid_ref[...])
    both = mm(xh, wcat[...]) + mm(xl, wcat[...])
    high, low = split(both[:, :hid] + both[:, hid:])
    here = pl.ds(pl.multiple_of(step * rows, rows), rows)
    gcat[here, :hid] = high
    gcat[here, hid:] = low

    @pl.when(step == steps - 1)
    def _():
        first = lax.axis_index("nodes") * blocks
        group = 4

        def body(i, carry):
            hots, messages = [], []
            for k in range(group):
                t = i * group + k
                tile = tiles[t, 0]
                live = tile >= 0
                block = jnp.where(live, tile - first, 0)
                ids = edges_ref[t]
                source = one_hot_rows(ids[0:1])
                target = one_hot_rows(ids[1:2])
                picked = jnp.concatenate([source, target], axis=1)
                block_rows = gcat[pl.ds(pl.multiple_of(block * BLOCK, BLOCK), BLOCK), :]
                table = jnp.concatenate([block_rows, mcat[...]], axis=0)
                pre = mm(picked, table)
                mh, ml = split(silu(pre[:, :hid] + pre[:, hid:]))
                messages.append(jnp.concatenate([mh, ml], axis=1))
                hots.append(one_hot_cols(jnp.where(live, ids[1:2], -1)))
            acc[...] += mm(jnp.concatenate(hots, axis=1), jnp.concatenate(messages, axis=0))
            return carry

        lax.fori_loop(0, slots // group, body, 0)
        out_ref[...] = acc[:, :hid] + acc[:, hid:]


def encoder(grid_latent, mesh_latent, enc_grid_w, enc_mesh_w, enc_tiles, enc_edges):
    rows, width = grid_latent.shape
    hid = enc_grid_w.shape[1]
    nodes = mesh_latent.shape[0]
    chunk = 512
    return pl.pallas_call(
        encoder_kernel,
        grid_spec=pltpu.PrefetchScalarGridSpec(
            num_scalar_prefetch=1,
            grid=(rows // chunk,),
            in_specs=[
                pl.BlockSpec((chunk, width), lambda i, t: (i, 0)),
                pl.BlockSpec((width, hid), lambda i, t: (0, 0)),
                pl.BlockSpec((nodes, width), lambda i, t: (0, 0)),
                pl.BlockSpec((width, hid), lambda i, t: (0, 0)),
                pl.BlockSpec(enc_edges.shape, lambda i, t: (0, 0, 0)),
            ],
            out_specs=pl.BlockSpec((nodes, hid), lambda i, t: (0, 0)),
            scratch_shapes=[
                pltpu.VMEM((width, 2 * hid), BF16),
                pltpu.VMEM((rows, 2 * hid), BF16),
                pltpu.VMEM((nodes, 2 * hid), BF16),
                pltpu.VMEM((nodes, 2 * hid), F32),
            ],
        ),
        out_shape=jax.ShapeDtypeStruct((nodes, hid), F32),
        compiler_params=pltpu.CompilerParams(vmem_limit_bytes=40 << 20),
        cost_estimate=pl.CostEstimate(
            flops=2 * 6 * rows * width * hid, bytes_accessed=6 << 20, transcendentals=1 << 20
        ),
        name="encoder",
    )(enc_tiles, grid_latent, enc_grid_w, mesh_latent, enc_mesh_w, enc_edges)


def decoder_kernel(
    tiles, grid_ref, wg_ref, mesh_ref, wo_ref, edges_ref, out_ref, gcat, mcat, wcat, agg
):
    rows, width = grid_ref.shape
    hid = wg_ref.shape[1]
    blocks = rows // BLOCK
    mp = lax.axis_size("mp")
    node = lax.axis_index("nodes")
    nodes = lax.axis_size("nodes")
    first = (node * mp + lax.axis_index("mp")) * blocks

    wh, wl = split(wg_ref[...])
    wcat[:, :hid] = wh
    wcat[:, hid:] = wl
    for b in range(blocks):
        here = slice(b * BLOCK, (b + 1) * BLOCK)
        xh, xl = split(grid_ref[here, :])
        high, low = split(mm(xh, wcat[:, :hid]) + mm(xh, wcat[:, hid:]) + mm(xl, wcat[:, :hid]))
        gcat[here, :hid] = high
        gcat[here, hid:] = low
    high, low = split(mesh_ref[...])
    mcat[:, :hid] = high
    mcat[:, hid:] = low
    agg[...] = jnp.zeros_like(agg)

    def body(t, carry):
        block = tiles[t, 1] - first

        @pl.when(jnp.logical_and(block >= 0, block < blocks))
        def _():
            beside = lax.rem(tiles[t, 0] - (node - 1) + nodes, nodes)
            ids = edges_ref[t]
            source = one_hot_rows(ids[0:1])
            target = one_hot_rows(ids[1:2])
            picked = jnp.concatenate([source, target], axis=1)
            here = pl.ds(pl.multiple_of(block * BLOCK, BLOCK), BLOCK)
            there = pl.ds(pl.multiple_of(beside * BLOCK, BLOCK), BLOCK)
            table = jnp.concatenate([mcat[there, :], gcat[here, :]], axis=0)
            pre = mm(picked, table)
            mh, ml = split(silu(pre[:, :hid] + pre[:, hid:]))
            hot = one_hot_cols(ids[1:2])
            agg[here, :] += mm(hot, mh) + mm(hot, ml)

        return carry

    lax.fori_loop(0, edges_ref.shape[0], body, 0)
    wh, wl = split(wo_ref[...])
    for b in range(blocks):
        here = slice(b * BLOCK, (b + 1) * BLOCK)
        ah, al = split(agg[here, :])
        out_ref[here, :] = grid_ref[here, :] + (mm(ah, wh) + mm(ah, wl) + mm(al, wh))


def decoder(grid_latent, dec_grid_w, mesh_beside, dec_out_w, dec_tiles, dec_edges):
    rows, width = grid_latent.shape
    hid = dec_grid_w.shape[1]
    vmem = pl.BlockSpec(memory_space=pltpu.VMEM)
    share = rows // lax.axis_size("mp")
    me = lax.axis_index("mp")
    mine = lax.dynamic_slice_in_dim(grid_latent, me * share, share, 0)
    return pl.pallas_call(
        decoder_kernel,
        in_specs=[pl.BlockSpec(memory_space=pltpu.SMEM)] + [vmem] * 5,
        out_specs=vmem,
        out_shape=jax.ShapeDtypeStruct((share, width), F32),
        scratch_shapes=[
            pltpu.VMEM((share, 2 * hid), BF16),
            pltpu.VMEM((mesh_beside.shape[0], 2 * hid), BF16),
            pltpu.VMEM((width, 2 * hid), BF16),
            pltpu.VMEM((share, hid), F32),
        ],
        compiler_params=pltpu.CompilerParams(vmem_limit_bytes=40 << 20),
        cost_estimate=pl.CostEstimate(
            flops=2 * 6 * share * width * hid, bytes_accessed=6 << 20, transcendentals=1 << 20
        ),
        name="decoder",
    )(dec_tiles, mine, dec_grid_w, mesh_beside, dec_out_w, dec_edges)


def attention_kernel(listed, query_ref, near_ref, out_ref, scores, values):
    step = pl.program_id(0)
    near = near_ref[0]
    here = pl.ds(pl.multiple_of(step * BLOCK, BLOCK), BLOCK)
    scores[:, here] = lax.dot_general(
        query_ref[...],
        near[:, :HEAD_DIM],
        (((1,), (1,)), ((), ())),
        precision=FULL,
        preferred_element_type=F32,
    ) * (1.0 / math.sqrt(HEAD_DIM))
    values[here, :] = near[:, HEAD_DIM:]

    @pl.when(step == pl.num_programs(0) - 1)
    def _():
        logits = scores[...]
        weights = jnp.exp(logits - jnp.max(logits, axis=-1, keepdims=True))
        total = jnp.sum(weights, axis=-1, keepdims=True)
        out_ref[...] = product(weights, values[...]) / total


def attention(queries, everything, neighbor_blocks):
    listed = neighbor_blocks.shape[1]
    rows = queries.shape[0]
    return pl.pallas_call(
        attention_kernel,
        grid_spec=pltpu.PrefetchScalarGridSpec(
            num_scalar_prefetch=1,
            grid=(listed,),
            in_specs=[
                pl.BlockSpec((rows, HEAD_DIM), lambda i, t: (0, 0)),
                pl.BlockSpec(
                    (1, BLOCK, 2 * HEAD_DIM), lambda i, t: (t[lax.axis_index("nodes"), i], 0, 0)
                ),
            ],
            out_specs=pl.BlockSpec((rows, HEAD_DIM), lambda i, t: (0, 0)),
            scratch_shapes=[
                pltpu.VMEM((rows, listed * BLOCK), F32),
                pltpu.VMEM((listed * BLOCK, HEAD_DIM), F32),
            ],
        ),
        out_shape=jax.ShapeDtypeStruct((rows, HEAD_DIM), F32),
        compiler_params=pltpu.CompilerParams(vmem_limit_bytes=24 << 20),
        name="attention",
    )(neighbor_blocks, queries, everything)


def per_device(
    grid_latent,
    mesh_latent,
    enc_grid_w,
    enc_mesh_w,
    enc_out_w,
    block_gain,
    query_w,
    key_w,
    value_w,
    out_w,
    up_w,
    down_w,
    dec_gain,
    dec_grid_w,
    dec_mesh_w,
    dec_out_w,
    neighbor_blocks,
    enc_tiles,
    enc_edges,
    dec_tiles,
    dec_edges,
):
    me_node = lax.axis_index("nodes")
    count = lax.axis_size("nodes")
    node_rows = mesh_latent.shape[0]
    outs = jnp.concatenate([enc_out_w, out_w, dec_out_w], axis=1)
    outs = lax.all_gather(outs, "mp", axis=0, tiled=True)
    enc_out_all, out_all, dec_out_all = jnp.split(outs, 3, axis=1)
    dec_grid_all = lax.all_gather(dec_grid_w.T, "mp", axis=0, tiled=True).T
    dec_mesh_all = lax.all_gather(dec_mesh_w.T, "mp", axis=0, tiled=True).T

    enc_agg = encoder(grid_latent, mesh_latent, enc_grid_w, enc_mesh_w, enc_tiles, enc_edges)
    enc_agg = lax.all_gather(enc_agg, "mp", axis=1, tiled=True)
    mesh_one = mesh_latent + product(enc_agg, enc_out_all)
    normed = layer_norm(mesh_one, block_gain)
    queries = product(normed, query_w)
    key_values = jnp.concatenate([product(normed, key_w), product(normed, value_w)], axis=1)
    everything = lax.all_gather(key_values, "nodes", axis=0, tiled=False)
    hidden = jax.nn.silu(product(normed, up_w))
    mlp = lax.psum(product(hidden, down_w), "mp")
    attended = attention(queries, everything, neighbor_blocks)
    attended = lax.all_gather(attended, "mp", axis=1, tiled=True)
    mesh_two = mesh_one + mlp + product(attended, out_all)
    mesh_dec = product(layer_norm(mesh_two, dec_gain), dec_mesh_all)
    up = [(i, (i + 1) % count) for i in range(count)]
    down = [(j, i) for i, j in up]
    before = lax.ppermute(mesh_dec, "nodes", up)
    after = lax.ppermute(mesh_dec, "nodes", down)
    beside = jnp.concatenate([before, mesh_dec, after], axis=0)
    rows_out = decoder(grid_latent, dec_grid_all, beside, dec_out_all, dec_tiles, dec_edges)
    return lax.all_to_all(rows_out, "mp", split_axis=1, concat_axis=0, tiled=True)


def solution(mesh):
    in_specs = (
        P("nodes", None),
        P("nodes", None),
        P(None, "mp"),
        P(None, "mp"),
        P("mp", None),
        P(),
        P(None, "mp"),
        P(None, "mp"),
        P(None, "mp"),
        P("mp", None),
        P(None, "mp"),
        P("mp", None),
        P(),
        P(None, "mp"),
        P(None, "mp"),
        P("mp", None),
        P(),
        P("nodes", None),
        P("nodes", None, None),
        P("nodes", None),
        P("nodes", None, None),
    )
    out_specs = P("nodes", "mp")
    return jax.shard_map(
        per_device, mesh=mesh, in_specs=in_specs, out_specs=out_specs, check_vma=False
    )
```

```python
import math

import jax
import jax.numpy as jnp
from jax import lax
from jax.experimental import pallas as pl
from jax.experimental.pallas import tpu as pltpu
from jax.sharding import PartitionSpec as P

HEAD_DIM = 128
BLOCK = 128
FULL = lax.Precision.HIGHEST
F32 = jnp.float32
BF16 = jnp.bfloat16


def product(matrix, weight):
    return jnp.dot(matrix, weight, precision=FULL, preferred_element_type=F32)


def split(x):
    high = x.astype(BF16)
    low = (x - high.astype(F32)).astype(BF16)
    return high, low


def mm(a, b):
    return jnp.dot(a, b, preferred_element_type=F32)


def silu(v):
    return v * (1.0 / (1.0 + jnp.exp(-v)))


def as_column(row):
    return jnp.broadcast_to(row, (8, BLOCK)).T[:, 0:1]


def one_hot_rows(row):
    lane = lax.broadcasted_iota(jnp.int32, (BLOCK, BLOCK), 1)
    return jnp.where(as_column(row) == lane, 1.0, 0.0).astype(BF16)


def one_hot_cols(row):
    sub = lax.broadcasted_iota(jnp.int32, (BLOCK, BLOCK), 0)
    return jnp.where(row == sub, 1.0, 0.0).astype(BF16)


MESH = pl.DeviceIdType.MESH
Z, X, MP = 8, 4, 4
CHIPS = Z * X
CHUNKS = ((0, 40), (40, 40), (80, 24), (104, 24))


def spans(chunk):
    plus = chunk % 2 == 0
    zs = (-3, 4) if plus else (-4, 3)
    xs = (-1, 2) if plus else (-2, 1)
    return zs, xs


def onward(chunk, dz, dx):
    zs, xs = spans(chunk)
    steps = []

    def along_z(start):
        if dz >= 0 and dz + 1 <= zs[1] and (start or dz > 0):
            steps.append((1, 0))
        if dz <= 0 and dz - 1 >= zs[0] and (start or dz < 0):
            steps.append((-1, 0))

    def along_x(start):
        if dx >= 0 and dx + 1 <= xs[1] and (start or dx > 0):
            steps.append((0, 1))
        if dx <= 0 and dx - 1 >= xs[0] and (start or dx < 0):
            steps.append((0, -1))

    if chunk < 2:
        if dx == 0:
            along_z(dz == 0)
            along_x(True)
        else:
            along_x(False)
    else:
        if dz == 0:
            along_x(dx == 0)
            along_z(True)
        else:
            along_z(False)
    return steps


def arrivals():
    events = []
    for chunk in range(4):
        zs, xs = spans(chunk)
        for dz in range(zs[0], zs[1] + 1):
            for dx in range(xs[0], xs[1] + 1):
                if (dz, dx) != (0, 0):
                    slot = (dz - zs[0]) * X + dx - xs[0]
                    events.append((abs(dz) + abs(dx), abs(dz), chunk, dz, dx, slot))
    return sorted(events)


def slot_of(chunk, dz, dx):
    zs, xs = spans(chunk)
    return (dz - zs[0]) * X + dx - xs[0]


def norm_rows(x, gain):
    centre = jnp.mean(x, axis=-1, keepdims=True)
    shifted = x - centre
    spread = jnp.mean(shifted * shifted, axis=-1, keepdims=True)
    return shifted * lax.rsqrt(spread + 1e-05) * gain


def mm3(ah, al, bh, bl):
    return mm(ah, bh) + mm(ah, bl) + mm(al, bh)


def mesh_kernel(
    tiles,
    lists,
    grid_ref,
    mesh_ref,
    enc_grid_w,
    enc_mesh_w,
    enc_edges,
    enc_out_w,
    gain_one,
    query_w,
    key_w,
    value_w,
    out_w,
    up_w,
    down_w,
    gain_two,
    dec_grid_w,
    dec_mesh_w,
    dec_out_w,
    beside,
    dec_grid_all,
    dec_out_all,
    wcat,
    gcat,
    mcat,
    acc,
    agg_all,
    enc_out_all,
    out_all,
    dec_mesh_all,
    kv,
    partial,
    parts,
    summed,
    att_all,
    scores,
    y_send,
    y_recv,
    c_send,
    c_recv,
    link_send,
    link_recv,
    core_send,
    core_recv,
    side_send,
    side_recv,
):
    me = lax.axis_index("mp")
    node = lax.axis_index("nodes")
    nodes = Z * X * 2
    core = lax.rem(node, 2)
    chip = node // 2
    z, x = chip // X, lax.rem(chip, X)
    z_at = {d: lax.rem(z + d + 2 * Z, Z) for d in range(-4, 5)}
    x_at = {d: lax.rem(x + d + 2 * X, X) for d in range(-2, 3)}
    sibling = node + 1 - 2 * core
    y_at = [lax.rem(me + k, MP) for k in range(MP)]
    y_from = [lax.rem(me + MP - k, MP) for k in range(MP)]
    after, before = lax.rem(node + 1, nodes), lax.rem(node + nodes - 1, nodes)
    beyond = jnp.where(core == 0, before, after)

    def chip_node(dz, dx):
        return (z_at[dz] * X + x_at[dx]) * 2 + core

    barrier = pltpu.get_barrier_semaphore()
    for dz, dx in ((1, 0), (-1, 0), (0, 1), (0, -1)):
        pl.semaphore_signal(
            barrier, inc=1, device_id={"nodes": chip_node(dz, dx)}, device_id_type=MESH
        )
    pl.semaphore_signal(barrier, inc=1, device_id={"nodes": sibling}, device_id_type=MESH)
    pl.semaphore_signal(barrier, inc=1, device_id={"nodes": beyond}, device_id_type=MESH)
    for k in range(1, MP):
        pl.semaphore_signal(barrier, inc=1, device_id={"mp": y_at[k]}, device_id_type=MESH)
    pl.semaphore_wait(barrier, 9)

    def y_copy(item, k, src, dst):
        return pltpu.make_async_remote_copy(
            src_ref=src,
            dst_ref=dst,
            send_sem=y_send.at[item, k - 1],
            recv_sem=y_recv.at[item, k - 1],
            device_id={"mp": y_at[k]},
            device_id_type=MESH,
        )

    def c_copy(item, k, ref):
        return pltpu.make_async_remote_copy(
            src_ref=ref,
            dst_ref=ref,
            send_sem=c_send.at[item, k - 1],
            recv_sem=c_recv.at[item, k - 1],
            device_id={"nodes": sibling},
            device_id_type=MESH,
        )

    weights = {
        0: (enc_out_w, enc_out_all),
        1: (dec_grid_w, dec_grid_all),
        2: (out_w, out_all),
        3: (dec_mesh_w, dec_mesh_all),
        4: (dec_out_w, dec_out_all),
    }

    def halves(item):
        half = weights[item][0].shape[0] // 2
        return pl.ds(pl.multiple_of(core * half, half), half), pl.ds(
            pl.multiple_of((1 - core) * half, half), half
        )

    def weight_start(item):
        own, whole = weights[item]
        mine, _ = halves(item)
        for k in range(1, MP):
            y_copy(item, k, own.at[mine], whole.at[me, mine]).start()
        whole[me] = own[...]

    def weight_pass_on(item):
        own, whole = weights[item]
        mine, _ = halves(item)
        for k in range(1, MP):
            y_copy(item, k, own.at[mine], whole.at[y_from[k], mine]).wait_recv()
            c_copy(item, k, whole.at[y_from[k], mine]).start()

    def weight_finish(item):
        own, whole = weights[item]
        mine, other = halves(item)
        for k in range(1, MP):
            c_copy(item, k, whole.at[y_from[k], other]).wait_recv()
        for k in range(1, MP):
            y_copy(item, k, own.at[mine], whole.at[me, mine]).wait_send()
            c_copy(item, k, whole.at[y_from[k], mine]).wait_send()

    weight_start(0)
    weight_start(1)

    rows, hid = grid_ref.shape[0], enc_grid_w.shape[1]
    blocks = rows // BLOCK
    slots = enc_edges.shape[0]
    high, low = split(enc_grid_w[...])
    wcat[:, :hid] = high
    wcat[:, hid:] = low
    high, low = split(product(mesh_ref[...], enc_mesh_w[...]))
    mcat[:, :hid] = high
    mcat[:, hid:] = low
    acc[...] = jnp.zeros_like(acc)
    chunk_rows = 256

    def project(i, carry):
        here = pl.ds(pl.multiple_of(i * chunk_rows, chunk_rows), chunk_rows)
        xh, xl = split(grid_ref[here, :])
        both = mm(xh, wcat[...]) + mm(xl, wcat[...])
        high, low = split(both[:, :hid] + both[:, hid:])
        for j in range(chunk_rows // BLOCK):
            part = slice(j * BLOCK, (j + 1) * BLOCK)
            gcat[i * (chunk_rows // BLOCK) + j, :, :hid] = high[part]
            gcat[i * (chunk_rows // BLOCK) + j, :, hid:] = low[part]
        return carry

    lax.fori_loop(0, rows // chunk_rows, project, 0)
    first = node * blocks
    group = 4

    def edges(i, carry):
        hots, messages = [], []
        for k in range(group):
            t = i * group + k
            tile = tiles[t, 0]
            live = tile >= 0
            block = jnp.clip(tile - first, 0, blocks - 1)
            ids = enc_edges[t]
            source = one_hot_rows(ids[0:1])
            target = one_hot_rows(ids[1:2])
            picked = jnp.concatenate([source, target], axis=1)
            table = jnp.concatenate([gcat[block], mcat[...]], axis=0)
            pre = mm(picked, table)
            mh, ml = split(silu(pre[:, :hid] + pre[:, hid:]))
            messages.append(jnp.concatenate([mh, ml], axis=1))
            hots.append(one_hot_cols(jnp.where(live, ids[1:2], -1)))
        acc[...] += mm(jnp.concatenate(hots, axis=1), jnp.concatenate(messages, axis=0))
        return carry

    half_way = slots // group // 2
    lax.fori_loop(0, half_way, edges, 0)
    weight_pass_on(0)
    lax.fori_loop(half_way, slots // group, edges, 0)
    agg_all[me] = acc[:, :hid] + acc[:, hid:]
    for k in range(1, MP):
        y_copy(5, k, agg_all.at[me], agg_all.at[me]).start()
    weight_finish(0)
    weight_pass_on(1)
    for k in range(1, MP):
        y_copy(5, k, agg_all.at[me], agg_all.at[y_from[k]]).wait_recv()
    agg = jnp.concatenate([agg_all[m] for m in range(MP)], axis=1)
    width = mesh_ref.shape[1]
    mesh_one = mesh_ref[...] + product(agg, enc_out_all[...].reshape(width, width))
    normed = norm_rows(mesh_one, gain_one[...])
    own_kv = product(normed, jnp.concatenate([key_w[...], value_w[...]], axis=1))
    here = core * CHIPS + chip
    kv[here] = own_kv

    def link_copy(chunk, pos, slot, step):
        start, size = CHUNKS[chunk]
        piece = kv.at[pos, pl.ds(start, size)]
        return pltpu.make_async_remote_copy(
            src_ref=piece,
            dst_ref=piece,
            send_sem=link_send,
            recv_sem=link_recv.at[chunk, slot],
            device_id={"nodes": chip_node(*step)},
            device_id_type=MESH,
        )

    def core_copy(ref):
        return pltpu.make_async_remote_copy(
            src_ref=ref,
            dst_ref=ref,
            send_sem=core_send,
            recv_sem=core_recv,
            device_id={"nodes": sibling},
            device_id_type=MESH,
        )

    for chunk in range(4):
        for step in onward(chunk, 0, 0):
            link_copy(chunk, here, slot_of(chunk, *step), step).start()
    core_copy(kv.at[here]).start()

    def arrive(event):
        _, _, chunk, dz, dx, slot = event
        pos = core * CHIPS + z_at[-dz] * X + x_at[-dx]
        start, size = CHUNKS[chunk]
        link_copy(chunk, pos, slot, (1, 0)).wait_recv()
        for step in onward(chunk, dz, dx):
            link_copy(
                chunk, pos, slot_of(chunk, dz + step[0], dx + step[1]), step
            ).start()
        core_copy(kv.at[pos, pl.ds(start, size)]).start()

    nh, nl = split(normed)
    uh, ul = split(up_w[...])
    hidden = silu(mm3(nh, nl, uh, ul))
    queue = arrivals()
    near = [e for e in queue if e[0] == 1]
    rest = [e for e in queue if e[0] > 1]
    for event in near:
        arrive(event)
    hh, hl = split(hidden)
    dh, dl = split(down_w[...])
    partial[...] = mm3(hh, hl, dh, dl)
    share = BLOCK // MP

    def share_of(m):
        return pl.ds(pl.multiple_of(m * share, share), share)

    for k in range(1, MP):
        y_copy(6, k, partial.at[share_of(y_at[k])], parts.at[me]).start()
    for item in (2, 3, 4):
        weight_start(item)
    third = len(rest) // 4
    for event in rest[:third]:
        arrive(event)
    weight_finish(1)
    for k in range(1, MP):
        y_copy(6, k, partial.at[share_of(y_at[k])], parts.at[y_from[k]]).wait_recv()
    summed[share_of(me), :] = partial[share_of(me), :] + (
        parts[y_from[1]] + parts[y_from[2]] + parts[y_from[3]]
    )
    for k in range(1, MP):
        y_copy(7, k, summed.at[share_of(me)], summed.at[share_of(me)]).start()
    queries = product(normed, query_w[...]) * (1.0 / math.sqrt(HEAD_DIM))
    for event in rest[third : 2 * third]:
        arrive(event)
    weight_pass_on(2)
    for event in rest[2 * third : 3 * third]:
        arrive(event)
    weight_pass_on(3)
    for event in rest[3 * third :]:
        arrive(event)
    weight_pass_on(4)
    for k in range(1, MP):
        y_copy(7, k, summed.at[share_of(me)], summed.at[share_of(y_from[k])]).wait_recv()
    mesh_mid = mesh_one + summed[...]
    weight_finish(2)
    core_copy(kv.at[pl.ds((1 - core) * CHIPS, CHIPS)]).wait_recv()

    count = lists.shape[1]
    top = jnp.full((BLOCK, 1), -jnp.inf, F32)
    spots = []
    for j in range(count):
        block = lists[node, j]
        spot = jnp.bitwise_and(block, 1) * CHIPS + jnp.right_shift(block, 1)
        spots.append(spot)
        logit = lax.dot_general(
            queries,
            kv[spot][:, :HEAD_DIM],
            (((1,), (1,)), ((), ())),
            precision=FULL,
            preferred_element_type=F32,
        )
        scores[:, j * BLOCK : (j + 1) * BLOCK] = logit
        top = jnp.maximum(top, jnp.max(logit, axis=-1, keepdims=True))
    weight = jnp.exp(scores[...] - top)
    total = jnp.sum(weight, axis=-1, keepdims=True)
    values = jnp.concatenate([kv[spot][:, HEAD_DIM:] for spot in spots], axis=0)
    wh, wl = split(weight)
    vh, vl = split(values)
    att_all[me] = mm3(wh, wl, vh, vl) / total
    for k in range(1, MP):
        y_copy(8, k, att_all.at[me], att_all.at[me]).start()
    weight_finish(3)
    for k in range(1, MP):
        y_copy(8, k, att_all.at[me], att_all.at[y_from[k]]).wait_recv()
    attended = jnp.concatenate([att_all[m] for m in range(MP)], axis=1)
    mesh_two = mesh_mid + product(attended, out_all[...].reshape(width, width))
    normed_two = norm_rows(mesh_two, gain_two[...])
    dec_w = jnp.concatenate([dec_mesh_all[m] for m in range(MP)], axis=1)
    beside[1] = product(normed_two, dec_w)

    def side_copy(way, slot, target):
        return pltpu.make_async_remote_copy(
            src_ref=beside.at[1],
            dst_ref=beside.at[slot],
            send_sem=side_send.at[way],
            recv_sem=side_recv.at[way],
            device_id={"nodes": target},
            device_id_type=MESH,
        )

    side_copy(0, 0, after).start()
    side_copy(1, 2, before).start()
    weight_finish(4)
    core_copy(kv.at[pl.ds(core * CHIPS, CHIPS)]).wait_send()
    link_copy_all = pltpu.make_async_remote_copy(
        src_ref=kv.at[pl.ds(0, CHIPS - 1)],
        dst_ref=kv.at[pl.ds(0, CHIPS - 1)],
        send_sem=link_send,
        recv_sem=link_recv.at[0, 0],
        device_id={"nodes": sibling},
        device_id_type=MESH,
    )
    link_copy_all.wait_send()
    for item, ref in ((5, agg_all.at[me]), (8, att_all.at[me])):
        for k in range(1, MP):
            y_copy(item, k, ref, ref).wait_send()
    for item in (6, 7):
        for k in range(1, MP):
            ref = summed.at[share_of(me)]
            y_copy(item, k, ref, ref).wait_send()
    side_copy(0, 0, after).wait()
    side_copy(1, 2, before).wait()


def mesh_part(tiles, lists, *arrays):
    grid_latent, mesh_latent, enc_grid_w = arrays[:3]
    rows, width = grid_latent.shape
    nodes = mesh_latent.shape[0]
    hid = enc_grid_w.shape[1]
    vmem = pl.BlockSpec(memory_space=pltpu.VMEM)
    smem = pl.BlockSpec(memory_space=pltpu.SMEM)
    dma = pltpu.SemaphoreType.DMA
    listed = lists.shape[1]
    return pl.pallas_call(
        mesh_kernel,
        in_specs=[smem, smem] + [vmem] * len(arrays),
        out_specs=[vmem] * 3,
        out_shape=[
            jax.ShapeDtypeStruct((3, nodes, width), F32),
            jax.ShapeDtypeStruct((MP, width, hid), F32),
            jax.ShapeDtypeStruct((MP, hid, width), F32),
        ],
        scratch_shapes=[
            pltpu.VMEM((width, 2 * hid), BF16),
            pltpu.VMEM((rows // BLOCK, BLOCK, 2 * hid), BF16),
            pltpu.VMEM((nodes, 2 * hid), BF16),
            pltpu.VMEM((nodes, 2 * hid), F32),
            pltpu.VMEM((MP, nodes, hid), F32),
            pltpu.VMEM((MP, hid, width), F32),
            pltpu.VMEM((MP, hid, width), F32),
            pltpu.VMEM((MP, width, hid), F32),
            pltpu.VMEM((2 * CHIPS, nodes, 2 * HEAD_DIM), F32),
            pltpu.VMEM((nodes, width), F32),
            pltpu.VMEM((MP, nodes // MP, width), F32),
            pltpu.VMEM((nodes, width), F32),
            pltpu.VMEM((MP, nodes, HEAD_DIM), F32),
            pltpu.VMEM((nodes, listed * BLOCK), F32),
            dma((9, MP - 1)),
            dma((9, MP - 1)),
            dma((5, MP - 1)),
            dma((5, MP - 1)),
            dma(()),
            dma((4, CHIPS)),
            dma(()),
            dma(()),
            dma((2,)),
            dma((2,)),
        ],
        compiler_params=pltpu.CompilerParams(
            collective_id=0, has_side_effects=True, vmem_limit_bytes=52 << 20
        ),
        name="mesh_part",
    )(tiles, lists, *arrays)


def exchange_kernel(rows_ref, out_ref, send, recv, local):
    me = lax.axis_index("mp")
    share = rows_ref.shape[1]
    y_at = [lax.rem(me + k, MP) for k in range(MP)]
    y_from = [lax.rem(me + MP - k, MP) for k in range(MP)]
    barrier = pltpu.get_barrier_semaphore()
    for k in range(1, MP):
        pl.semaphore_signal(barrier, inc=1, device_id={"mp": y_at[k]}, device_id_type=MESH)
    pl.semaphore_wait(barrier, MP - 1)

    def place(m):
        return pl.ds(pl.multiple_of(m * share, share), share)

    def copy(k, at):
        return pltpu.make_async_remote_copy(
            src_ref=rows_ref.at[y_at[k]],
            dst_ref=out_ref.at[place(at)],
            send_sem=send.at[k - 1],
            recv_sem=recv.at[k - 1],
            device_id={"mp": y_at[k]},
            device_id_type=MESH,
        )

    for k in (2, 1, 3):
        copy(k, me).start()
    own = pltpu.make_async_copy(rows_ref.at[me], out_ref.at[place(me)], local)
    own.start()
    own.wait()
    for k in range(1, MP):
        copy(k, y_from[k]).wait_recv()
        copy(k, me).wait_send()


def exchange(rows):
    dma = pltpu.SemaphoreType.DMA
    anywhere = pl.BlockSpec(memory_space=pl.ANY)
    return pl.pallas_call(
        exchange_kernel,
        in_specs=[anywhere],
        out_specs=anywhere,
        out_shape=jax.ShapeDtypeStruct((MP * rows.shape[1], rows.shape[2]), F32),
        scratch_shapes=[dma((MP - 1,)), dma((MP - 1,)), dma(())],
        compiler_params=pltpu.CompilerParams(collective_id=1, has_side_effects=True),
        name="exchange",
    )(rows)


def decoder_kernel(
    tiles, grid_ref, wg_ref, mesh_ref, wo_ref, edges_ref, out_ref, gcat, mcat, wcat, agg
):
    rows, width = grid_ref.shape
    hid = width
    blocks = rows // BLOCK
    mp = lax.axis_size("mp")
    node = lax.axis_index("nodes")
    nodes = lax.axis_size("nodes")
    first = (node * mp + lax.axis_index("mp")) * blocks

    wh, wl = split(jnp.concatenate([wg_ref[m] for m in range(MP)], axis=1))
    wcat[:, :hid] = wh
    wcat[:, hid:] = wl
    for b in range(blocks):
        here = slice(b * BLOCK, (b + 1) * BLOCK)
        xh, xl = split(grid_ref[here, :])
        high, low = split(mm(xh, wcat[:, :hid]) + mm(xh, wcat[:, hid:]) + mm(xl, wcat[:, :hid]))
        gcat[here, :hid] = high
        gcat[here, hid:] = low
    high, low = split(mesh_ref[...].reshape(-1, width))
    mcat[:, :hid] = high
    mcat[:, hid:] = low
    agg[...] = jnp.zeros_like(agg)

    def body(t, carry):
        block = tiles[t, 1] - first

        @pl.when(jnp.logical_and(block >= 0, block < blocks))
        def _():
            beside = lax.rem(tiles[t, 0] - (node - 1) + nodes, nodes)
            ids = edges_ref[t]
            source = one_hot_rows(ids[0:1])
            target = one_hot_rows(ids[1:2])
            picked = jnp.concatenate([source, target], axis=1)
            here = pl.ds(pl.multiple_of(block * BLOCK, BLOCK), BLOCK)
            there = pl.ds(pl.multiple_of(beside * BLOCK, BLOCK), BLOCK)
            table = jnp.concatenate([mcat[there, :], gcat[here, :]], axis=0)
            pre = mm(picked, table)
            mh, ml = split(silu(pre[:, :hid] + pre[:, hid:]))
            hot = one_hot_cols(ids[1:2])
            agg[here, :] += mm(hot, mh) + mm(hot, ml)

        return carry

    lax.fori_loop(0, edges_ref.shape[0], body, 0)
    wh, wl = split(wo_ref[...].reshape(hid, width))
    for b in range(blocks):
        here = slice(b * BLOCK, (b + 1) * BLOCK)
        ah, al = split(agg[here, :])
        done = grid_ref[here, :] + mm3(ah, al, wh, wl)
        for m in range(MP):
            out_ref[m, here, :] = done[:, m * (width // MP) : (m + 1) * (width // MP)]


def decoder(grid_latent, dec_grid_w, mesh_beside, dec_out_w, dec_tiles, dec_edges):
    rows, width = grid_latent.shape
    hid = width
    vmem = pl.BlockSpec(memory_space=pltpu.VMEM)
    share = rows // lax.axis_size("mp")
    me = lax.axis_index("mp")
    mine = lax.dynamic_slice_in_dim(grid_latent, me * share, share, 0)
    return pl.pallas_call(
        decoder_kernel,
        in_specs=[pl.BlockSpec(memory_space=pltpu.SMEM)] + [vmem] * 5,
        out_specs=vmem,
        out_shape=jax.ShapeDtypeStruct((MP, share, width // MP), F32),
        scratch_shapes=[
            pltpu.VMEM((share, 2 * hid), BF16),
            pltpu.VMEM((3 * BLOCK, 2 * hid), BF16),
            pltpu.VMEM((width, 2 * hid), BF16),
            pltpu.VMEM((share, hid), F32),
        ],
        compiler_params=pltpu.CompilerParams(vmem_limit_bytes=40 << 20),
        cost_estimate=pl.CostEstimate(
            flops=2 * 6 * share * width * hid, bytes_accessed=6 << 20, transcendentals=1 << 20
        ),
        name="decoder",
    )(dec_tiles, mine, dec_grid_w, mesh_beside, dec_out_w, dec_edges)


def per_device(
    grid_latent,
    mesh_latent,
    enc_grid_w,
    enc_mesh_w,
    enc_out_w,
    block_gain,
    query_w,
    key_w,
    value_w,
    out_w,
    up_w,
    down_w,
    dec_gain,
    dec_grid_w,
    dec_mesh_w,
    dec_out_w,
    neighbor_blocks,
    enc_tiles,
    enc_edges,
    dec_tiles,
    dec_edges,
):
    beside, dec_grid_all, dec_out_all = mesh_part(
        enc_tiles,
        neighbor_blocks,
        grid_latent,
        mesh_latent,
        enc_grid_w,
        enc_mesh_w,
        enc_edges,
        enc_out_w,
        block_gain[None],
        query_w,
        key_w,
        value_w,
        out_w,
        up_w,
        down_w,
        dec_gain[None],
        dec_grid_w,
        dec_mesh_w,
        dec_out_w,
    )
    rows = decoder(grid_latent, dec_grid_all, beside, dec_out_all, dec_tiles, dec_edges)
    return exchange(rows)


def solution(mesh):
    in_specs = (
        P("nodes", None),
        P("nodes", None),
        P(None, "mp"),
        P(None, "mp"),
        P("mp", None),
        P(),
        P(None, "mp"),
        P(None, "mp"),
        P(None, "mp"),
        P("mp", None),
        P(None, "mp"),
        P("mp", None),
        P(),
        P(None, "mp"),
        P(None, "mp"),
        P("mp", None),
        P(),
        P("nodes", None),
        P("nodes", None, None),
        P("nodes", None),
        P("nodes", None, None),
    )
    out_specs = P("nodes", "mp")
    return jax.shard_map(
        per_device, mesh=mesh, in_specs=in_specs, out_specs=out_specs, check_vma=False
    )
```

```python
import math

import jax
import jax.numpy as jnp
from jax import lax
from jax.experimental import pallas as pl
from jax.experimental.pallas import tpu as pltpu
from jax.sharding import PartitionSpec as P

HEAD_DIM = 128
BLOCK = 128
FULL = lax.Precision.HIGHEST
F32 = jnp.float32
BF16 = jnp.bfloat16


def product(matrix, weight):
    return jnp.dot(matrix, weight, precision=FULL, preferred_element_type=F32)


def split(x):
    high = x.astype(BF16)
    low = (x - high.astype(F32)).astype(BF16)
    return high, low


def mm(a, b):
    return jnp.dot(a, b, preferred_element_type=F32)


def mm_first(a, b):
    return lax.dot_general(a, b, (((0,), (0,)), ((), ())), preferred_element_type=F32)


def silu(v):
    half = 0.5 * v
    return half + half * jnp.tanh(half)


def one_hot_cols(row):
    sub = lax.broadcasted_iota(jnp.int32, (BLOCK, BLOCK), 0)
    return jnp.where(row == sub, 1.0, 0.0).astype(BF16)


MESH = pl.DeviceIdType.MESH
Z, X, MP = 8, 4, 4
CHIPS = Z * X
CHUNKS = ((0, 72), (72, 56))


def spans(chunk):
    return (1 - Z // 2, Z // 2), (1 - X // 2, X // 2)


def onward(chunk, dz, dx):
    zs, xs = spans(chunk)
    steps = []

    def along_z(start):
        if dz >= 0 and dz + 1 <= zs[1] and (start or dz > 0):
            steps.append((1, 0))
        if dz <= 0 and dz - 1 >= zs[0] and (start or dz < 0):
            steps.append((-1, 0))

    def along_x(start):
        if dx >= 0 and dx + 1 <= xs[1] and (start or dx > 0):
            steps.append((0, 1))
        if dx <= 0 and dx - 1 >= xs[0] and (start or dx < 0):
            steps.append((0, -1))

    if chunk == 0:
        if dx == 0:
            along_z(dz == 0)
            along_x(True)
        else:
            along_x(False)
    else:
        if dz == 0:
            along_x(dx == 0)
            along_z(True)
        else:
            along_z(False)
    return sorted(steps, key=lambda step: not branching(chunk, step))


def arrivals():
    events = []
    for chunk in range(len(CHUNKS)):
        zs, xs = spans(chunk)
        for dz in range(zs[0], zs[1] + 1):
            for dx in range(xs[0], xs[1] + 1):
                if (dz, dx) != (0, 0):
                    first, second = (dz, dx) if chunk == 0 else (dx, dz)
                    order = (abs(dz) + abs(dx), second != 0, abs(second))
                    events.append((order, chunk, dz, dx, slot_of(chunk, dz, dx)))
    return sorted(events)


def branching(chunk, step):
    return (step[0] != 0) == (chunk == 0)


def slot_of(chunk, dz, dx):
    zs, xs = spans(chunk)
    return (dz - zs[0]) * X + dx - xs[0]


def norm_rows(x, gain):
    centre = jnp.mean(x, axis=-1, keepdims=True)
    shifted = x - centre
    spread = jnp.mean(shifted * shifted, axis=-1, keepdims=True)
    return shifted * lax.rsqrt(spread + 1e-05) * gain


def mm3(ah, al, bh, bl):
    return mm(ah, bh) + mm(ah, bl) + mm(al, bh)


FETCHED = (
    "enc_grid_w",
    "mesh_latent",
    "enc_mesh_w",
    "enc_edges",
    "enc_out_w",
    "dec_grid_w",
    "block_gain",
    "key_w",
    "value_w",
    "up_w",
    "down_w",
    "query_w",
    "out_w",
    "dec_mesh_w",
    "dec_out_w",
    "dec_gain",
)


def mesh_kernel(tiles, lists, order, grid_hbm, *refs):
    count = len(FETCHED)
    given = dict(zip(FETCHED, refs[:count]))
    beside, gdec, dec_out_all = refs[count : count + 3]
    rest = refs[count + 3 :]
    held = dict(zip(FETCHED, rest[:count]))
    (
        grid_ref,
        wcat,
        gcat,
        mcat,
        acc,
        agg_all,
        enc_out_all,
        out_all,
        dec_mesh_all,
        dec_grid_all,
        kv,
        partial,
        parts,
        summed,
        att_all,
        scores,
        fetch_sem,
        grid_sem,
        y_send,
        y_recv,
        c_send,
        c_recv,
        link_send,
        link_recv,
        core_send,
        core_recv,
        side_send,
        side_recv,
    ) = rest[count:]
    chunk_rows = 256

    def fetch(name):
        return pltpu.make_async_copy(
            given[name], held[name], fetch_sem.at[FETCHED.index(name)]
        )

    def fetch_rows(i):
        here = pl.ds(pl.multiple_of(i * chunk_rows, chunk_rows), chunk_rows)
        there = pl.ds(i * (chunk_rows // BLOCK), chunk_rows // BLOCK)
        return pltpu.make_async_copy(
            grid_hbm.at[here].reshape(chunk_rows // BLOCK, BLOCK, grid_hbm.shape[1]),
            grid_ref.at[there],
            grid_sem.at[i],
        )

    for name in FETCHED[:3]:
        fetch(name).start()
    for i in range(grid_hbm.shape[0] // chunk_rows):
        fetch_rows(i).start()
    for name in FETCHED[3:]:
        fetch(name).start()

    def got(name):
        fetch(name).wait()
        return held[name][...]

    me = lax.axis_index("mp")
    node = lax.axis_index("nodes")
    nodes = Z * X * 2
    core = lax.rem(node, 2)
    chip = node // 2
    z, x = chip // X, lax.rem(chip, X)
    way = 1 - 2 * core
    z_at = {d: lax.rem(z + way * d + Z, Z) for d in range(-4, 5)}
    x_at = {d: lax.rem(x + way * d + X, X) for d in range(-2, 3)}
    sibling = node + way
    y_at = [lax.rem(me + k, MP) for k in range(MP)]
    y_from = [lax.rem(me + MP - k, MP) for k in range(MP)]
    after, before = lax.rem(node + 1, nodes), lax.rem(node + nodes - 1, nodes)
    beyond = jnp.where(core == 0, before, after)

    def chip_node(dz, dx):
        return (z_at[dz] * X + x_at[dx]) * 2 + core

    barrier = pltpu.get_barrier_semaphore()
    for dz, dx in ((1, 0), (-1, 0), (0, 1), (0, -1)):
        pl.semaphore_signal(
            barrier, inc=1, device_id={"nodes": chip_node(dz, dx)}, device_id_type=MESH
        )
    pl.semaphore_signal(barrier, inc=1, device_id={"nodes": sibling}, device_id_type=MESH)
    pl.semaphore_signal(barrier, inc=1, device_id={"nodes": beyond}, device_id_type=MESH)
    for k in range(1, MP):
        pl.semaphore_signal(barrier, inc=1, device_id={"mp": y_at[k]}, device_id_type=MESH)
    pl.semaphore_wait(barrier, 9)

    def y_copy(item, k, src, dst):
        return pltpu.make_async_remote_copy(
            src_ref=src,
            dst_ref=dst,
            send_sem=y_send.at[item, k - 1],
            recv_sem=y_recv.at[item, k - 1],
            device_id={"mp": y_at[k]},
            device_id_type=MESH,
        )

    def c_copy(item, k, ref):
        return pltpu.make_async_remote_copy(
            src_ref=ref,
            dst_ref=ref,
            send_sem=c_send.at[item, k - 1],
            recv_sem=c_recv.at[item, k - 1],
            device_id={"nodes": sibling},
            device_id_type=MESH,
        )

    weights = {
        0: ("enc_out_w", enc_out_all),
        1: ("dec_grid_w", dec_grid_all),
        2: ("out_w", out_all),
        3: ("dec_mesh_w", dec_mesh_all),
        4: ("dec_out_w", dec_out_all),
    }

    def halves(item):
        half = given[weights[item][0]].shape[0] // 2
        return pl.ds(pl.multiple_of(core * half, half), half), pl.ds(
            pl.multiple_of((1 - core) * half, half), half
        )

    def weight_start(item):
        name, whole = weights[item]
        own = given[name]
        mine, _ = halves(item)
        for k in range(1, MP):
            y_copy(item, k, own.at[mine], whole.at[me, mine]).start()

    def weight_pass_on(item):
        name, whole = weights[item]
        own = given[name]
        mine, _ = halves(item)
        for k in range(1, MP):
            y_copy(item, k, own.at[mine], whole.at[y_from[k], mine]).wait_recv()
            c_copy(item, k, whole.at[y_from[k], mine]).start()

    def weight_finish(item):
        name, whole = weights[item]
        own = given[name]
        mine, other = halves(item)
        whole[me] = got(name)
        for k in range(1, MP):
            c_copy(item, k, whole.at[y_from[k], other]).wait_recv()
        for k in range(1, MP):
            y_copy(item, k, own.at[mine], whole.at[me, mine]).wait_send()
            c_copy(item, k, whole.at[y_from[k], mine]).wait_send()

    weight_start(0)

    rows, hid = grid_hbm.shape[0], given["enc_grid_w"].shape[1]
    blocks = rows // BLOCK
    enc_edges = held["enc_edges"]
    slots = enc_edges.shape[0]
    high, low = split(got("enc_grid_w"))
    wcat[:, :hid] = high
    wcat[:, hid:] = low
    high, low = split(product(got("mesh_latent"), got("enc_mesh_w")))
    mcat[:, :hid] = high
    mcat[:, hid:] = low
    acc[...] = jnp.zeros_like(acc)

    def project(i, carry):
        fetch_rows(i).wait()
        there = pl.ds(i * (chunk_rows // BLOCK), chunk_rows // BLOCK)
        xh, xl = split(grid_ref[there].reshape(chunk_rows, -1))
        both = mm(xh, wcat[...]) + mm(xl, wcat[...])
        high, low = split(both[:, :hid] + both[:, hid:])
        for j in range(chunk_rows // BLOCK):
            part = slice(j * BLOCK, (j + 1) * BLOCK)
            gcat[i * (chunk_rows // BLOCK) + j, :, :hid] = high[part]
            gcat[i * (chunk_rows // BLOCK) + j, :, hid:] = low[part]
        return carry

    lax.fori_loop(0, rows // chunk_rows, project, 0)
    first = node * blocks
    group = 8

    def edges(i, carry):
        hots, messages = [], []
        for k in range(group):
            t = i * group + k
            tile = tiles[0, t]
            live = tile >= 0
            block = jnp.clip(tile - first, 0, blocks - 1)
            ids = enc_edges[t]
            target = one_hot_cols(ids[1:2])
            picked = jnp.concatenate([one_hot_cols(ids[0:1]), target], axis=0)
            table = jnp.concatenate([gcat[block], mcat[...]], axis=0)
            pre = mm_first(picked, table)
            mh, ml = split(silu(pre[:, :hid] + pre[:, hid:]))
            messages.append(jnp.concatenate([mh, ml], axis=1))
            hots.append(one_hot_cols(jnp.where(live, ids[1:2], -1)))
        acc[...] += mm(jnp.concatenate(hots, axis=1), jnp.concatenate(messages, axis=0))
        return carry

    half_way = slots // group // 2
    fetch("enc_edges").wait()
    lax.fori_loop(0, half_way, edges, 0)
    weight_pass_on(0)
    lax.fori_loop(half_way, slots // group, edges, 0)
    agg_all[me] = acc[:, :hid] + acc[:, hid:]
    for k in range(1, MP):
        y_copy(5, k, agg_all.at[me], agg_all.at[me]).start()
    weight_finish(0)
    for k in range(1, MP):
        y_copy(5, k, agg_all.at[me], agg_all.at[y_from[k]]).wait_recv()
    agg = jnp.concatenate([agg_all[m] for m in range(MP)], axis=1)
    width = grid_hbm.shape[1]
    mesh_one = held["mesh_latent"][...] + product(agg, enc_out_all[...].reshape(width, width))
    normed = norm_rows(mesh_one, got("block_gain"))
    own_kv = product(normed, jnp.concatenate([got("key_w"), got("value_w")], axis=1))
    here = core * CHIPS + chip
    kv[here] = own_kv

    def link_copy(chunk, pos, slot, step):
        start, size = CHUNKS[chunk]
        piece = kv.at[pos, pl.ds(start, size)]
        return pltpu.make_async_remote_copy(
            src_ref=piece,
            dst_ref=piece,
            send_sem=link_send,
            recv_sem=link_recv.at[chunk, slot],
            device_id={"nodes": chip_node(*step)},
            device_id_type=MESH,
        )

    def core_copy(ref):
        return pltpu.make_async_remote_copy(
            src_ref=ref,
            dst_ref=ref,
            send_sem=core_send,
            recv_sem=core_recv,
            device_id={"nodes": sibling},
            device_id_type=MESH,
        )

    starts = [(chunk, step) for chunk in range(len(CHUNKS)) for step in onward(chunk, 0, 0)]
    for chunk, step in sorted(starts, key=lambda s: not branching(*s)):
        link_copy(chunk, here, slot_of(chunk, *step), step).start()
    core_copy(kv.at[here]).start()
    weight_start(1)

    def arrive(event):
        _, chunk, dz, dx, slot = event
        pos = core * CHIPS + z_at[-dz] * X + x_at[-dx]
        start, size = CHUNKS[chunk]
        link_copy(chunk, pos, slot, (1, 0)).wait_recv()
        for step in onward(chunk, dz, dx):
            link_copy(
                chunk, pos, slot_of(chunk, dz + step[0], dx + step[1]), step
            ).start()
        core_copy(kv.at[pos, pl.ds(start, size)]).start()

    nh, nl = split(normed)
    uh, ul = split(got("up_w"))
    hidden = silu(mm3(nh, nl, uh, ul))
    queue = arrivals()
    near = [e for e in queue if e[0][0] == 1]
    rest = [e for e in queue if e[0][0] > 1]
    assert gdec.shape[0] == 4 * BLOCK
    for event in near:
        arrive(event)
    hh, hl = split(hidden)
    dh, dl = split(got("down_w"))
    partial[...] = mm3(hh, hl, dh, dl)
    share = BLOCK // MP

    def share_of(m):
        return pl.ds(pl.multiple_of(m * share, share), share)

    for k in range(1, MP):
        y_copy(6, k, partial.at[share_of(y_at[k])], parts.at[me]).start()
    for item in (2, 3, 4):
        weight_start(item)
    weight_pass_on(1)
    rest_count = len(rest)
    third = rest_count // 4
    for event in rest[:third]:
        arrive(event)
    weight_finish(1)
    gh, gl = split(jnp.concatenate([dec_grid_all[m] for m in range(MP)], axis=1))

    def grid_decode(b):
        block = jnp.clip(order[0, me * MP + b], 0, blocks - 1)
        xh, xl = split(grid_ref[block])
        high, low = split(mm3(xh, xl, gh, gl))
        gdec[b * BLOCK : (b + 1) * BLOCK, :width] = high
        gdec[b * BLOCK : (b + 1) * BLOCK, width:] = low

    grid_decode(0)
    for k in range(1, MP):
        y_copy(6, k, partial.at[share_of(y_at[k])], parts.at[y_from[k]]).wait_recv()
    summed[share_of(me), :] = partial[share_of(me), :] + (
        parts[y_from[1]] + parts[y_from[2]] + parts[y_from[3]]
    )
    for k in range(1, MP):
        y_copy(7, k, summed.at[share_of(me)], summed.at[share_of(me)]).start()
    queries = product(normed, got("query_w")) * (1.0 / math.sqrt(HEAD_DIM))
    for event in rest[third : 2 * third]:
        arrive(event)
    grid_decode(1)
    weight_pass_on(2)
    for event in rest[2 * third : 3 * third]:
        arrive(event)
    grid_decode(2)
    weight_pass_on(3)
    for event in rest[3 * third :]:
        arrive(event)
    weight_pass_on(4)
    grid_decode(3)
    for k in range(1, MP):
        y_copy(7, k, summed.at[share_of(me)], summed.at[share_of(y_from[k])]).wait_recv()
    mesh_mid = mesh_one + summed[...]
    weight_finish(2)
    core_copy(kv.at[pl.ds((1 - core) * CHIPS, CHIPS)]).wait_recv()

    count = lists.shape[0]
    top = jnp.full((BLOCK, 1), -jnp.inf, F32)
    spots = []
    for j in range(count):
        block = lists[j, node]
        spot = jnp.bitwise_and(block, 1) * CHIPS + jnp.right_shift(block, 1)
        spots.append(spot)
        logit = lax.dot_general(
            queries,
            kv[spot][:, :HEAD_DIM],
            (((1,), (1,)), ((), ())),
            precision=FULL,
            preferred_element_type=F32,
        )
        scores[:, j * BLOCK : (j + 1) * BLOCK] = logit
        top = jnp.maximum(top, jnp.max(logit, axis=-1, keepdims=True))
    weight = jnp.exp(scores[...] - top)
    total = jnp.sum(weight, axis=-1, keepdims=True)
    values = jnp.concatenate([kv[spot][:, HEAD_DIM:] for spot in spots], axis=0)
    wh, wl = split(weight)
    vh, vl = split(values)
    att_all[me] = mm3(wh, wl, vh, vl) / total
    for k in range(1, MP):
        y_copy(8, k, att_all.at[me], att_all.at[me]).start()
    weight_finish(3)
    for k in range(1, MP):
        y_copy(8, k, att_all.at[me], att_all.at[y_from[k]]).wait_recv()
    attended = jnp.concatenate([att_all[m] for m in range(MP)], axis=1)
    mesh_two = mesh_mid + mm3(*split(attended), *split(out_all[...].reshape(width, width)))
    normed_two = norm_rows(mesh_two, got("dec_gain"))
    dec_w = jnp.concatenate([dec_mesh_all[m] for m in range(MP)], axis=1)
    beside[1] = mm3(*split(normed_two), *split(dec_w))

    def side_copy(way, slot, target):
        return pltpu.make_async_remote_copy(
            src_ref=beside.at[1],
            dst_ref=beside.at[slot],
            send_sem=side_send.at[way],
            recv_sem=side_recv.at[way],
            device_id={"nodes": target},
            device_id_type=MESH,
        )

    side_copy(0, 0, after).start()
    side_copy(1, 2, before).start()
    weight_finish(4)
    core_copy(kv.at[pl.ds(core * CHIPS, CHIPS)]).wait_send()
    link_copy_all = pltpu.make_async_remote_copy(
        src_ref=kv.at[pl.ds(0, CHIPS - 1)],
        dst_ref=kv.at[pl.ds(0, CHIPS - 1)],
        send_sem=link_send,
        recv_sem=link_recv.at[0, 0],
        device_id={"nodes": sibling},
        device_id_type=MESH,
    )
    link_copy_all.wait_send()
    for item, ref in ((5, agg_all.at[me]), (8, att_all.at[me])):
        for k in range(1, MP):
            y_copy(item, k, ref, ref).wait_send()
    for item in (6, 7):
        for k in range(1, MP):
            ref = summed.at[share_of(me)]
            y_copy(item, k, ref, ref).wait_send()
    side_copy(0, 0, after).wait()
    side_copy(1, 2, before).wait()


def mesh_part(tiles, lists, order, grid_latent, arrays):
    rows, width = grid_latent.shape
    nodes = arrays["mesh_latent"].shape[0]
    hid = arrays["enc_grid_w"].shape[1]
    vmem = pl.BlockSpec(memory_space=pltpu.VMEM)
    smem = pl.BlockSpec(memory_space=pltpu.SMEM)
    hbm = pl.BlockSpec(memory_space=pltpu.HBM)
    dma = pltpu.SemaphoreType.DMA
    listed = lists.shape[0]
    operands = [arrays[name] for name in FETCHED]
    return pl.pallas_call(
        mesh_kernel,
        in_specs=[smem, smem, smem, hbm] + [hbm] * len(operands),
        out_specs=[vmem] * 3,
        out_shape=[
            jax.ShapeDtypeStruct((3, nodes, width), F32),
            jax.ShapeDtypeStruct((rows // MP, 2 * width), BF16),
            jax.ShapeDtypeStruct((MP, hid, width), F32),
        ],
        scratch_shapes=[pltpu.VMEM(array.shape, array.dtype) for array in operands]
        + [
            pltpu.VMEM((rows // BLOCK, BLOCK, width), F32),
            pltpu.VMEM((width, 2 * hid), BF16),
            pltpu.VMEM((rows // BLOCK, BLOCK, 2 * hid), BF16),
            pltpu.VMEM((nodes, 2 * hid), BF16),
            pltpu.VMEM((nodes, 2 * hid), F32),
            pltpu.VMEM((MP, nodes, hid), F32),
            pltpu.VMEM((MP, hid, width), F32),
            pltpu.VMEM((MP, hid, width), F32),
            pltpu.VMEM((MP, width, hid), F32),
            pltpu.VMEM((MP, width, hid), F32),
            pltpu.VMEM((2 * CHIPS, nodes, 2 * HEAD_DIM), F32),
            pltpu.VMEM((nodes, width), F32),
            pltpu.VMEM((MP, nodes // MP, width), F32),
            pltpu.VMEM((nodes, width), F32),
            pltpu.VMEM((MP, nodes, HEAD_DIM), F32),
            pltpu.VMEM((nodes, listed * BLOCK), F32),
            dma((len(operands),)),
            dma((rows // 256,)),
            dma((9, MP - 1)),
            dma((9, MP - 1)),
            dma((5, MP - 1)),
            dma((5, MP - 1)),
            dma(()),
            dma((len(CHUNKS), CHIPS)),
            dma(()),
            dma(()),
            dma((2,)),
            dma((2,)),
        ],
        compiler_params=pltpu.CompilerParams(
            collective_id=0, has_side_effects=True, vmem_limit_bytes=62 << 20
        ),
        name="mesh_part",
    )(tiles, lists, order, grid_latent, *operands)


def assign_kernel(tiles_ref, order_ref):
    blocks = MP * MP
    width = tiles_ref.shape[1]
    first = lax.axis_index("nodes") * blocks
    ids = tiles_ref[1:2, :] - first
    block = lax.broadcasted_iota(jnp.int32, (blocks, width), 0)
    tally = jnp.sum(jnp.where(ids == block, 1.0, 0.0), axis=1, keepdims=True)
    wide = jnp.broadcast_to(tally, (blocks, BLOCK))
    across = jnp.concatenate([wide] * (BLOCK // blocks), axis=0).T[:blocks, :blocks]
    down = wide[:, :blocks]
    i = lax.broadcasted_iota(jnp.int32, (blocks, blocks), 0)
    j = lax.broadcasted_iota(jnp.int32, (blocks, blocks), 1)
    ahead = jnp.logical_or(across > down, jnp.logical_and(across == down, j < i))
    rank = jnp.sum(jnp.where(ahead, 1.0, 0.0), axis=1, keepdims=True).astype(jnp.int32)
    device, turn = j // MP, lax.rem(j, MP)
    dealt = jnp.where(lax.rem(turn, 2) == 0, device, MP - 1 - device) + turn * MP
    chosen = jnp.where(rank == dealt, i.astype(F32), 0.0)
    order_ref[...] = jnp.sum(chosen, axis=0, keepdims=True).astype(jnp.int32)


def assign(dec_tiles):
    vmem = pl.BlockSpec(memory_space=pltpu.VMEM)
    return pl.pallas_call(
        assign_kernel,
        in_specs=[vmem],
        out_specs=vmem,
        out_shape=jax.ShapeDtypeStruct((1, MP * MP), jnp.int32),
        name="assign",
    )(dec_tiles)


def exchange_kernel(agg_hbm, wo_hbm, out_ref, agg, wo_ref, rows_ref, send, recv, fetch):
    me = lax.axis_index("mp")
    share, hid = agg_hbm.shape
    width = wo_hbm.shape[2] // MP
    blocks = share // BLOCK
    y_at = [lax.rem(me + k, MP) for k in range(MP)]
    y_from = [lax.rem(me + MP - k, MP) for k in range(MP)]

    def get(b):
        here = pl.ds(b * BLOCK, BLOCK)
        return pltpu.make_async_copy(agg_hbm.at[here], agg.at[here], fetch.at[b])

    get_wo = pltpu.make_async_copy(wo_hbm, wo_ref, fetch.at[blocks])
    get_wo.start()
    for b in range(blocks):
        get(b).start()
    barrier = pltpu.get_barrier_semaphore()
    for k in range(1, MP):
        pl.semaphore_signal(barrier, inc=1, device_id={"mp": y_at[k]}, device_id_type=MESH)
    get_wo.wait()
    wh, wl = split(wo_ref[...].reshape(hid, MP * width))

    def copy(b, k, at):
        return pltpu.make_async_remote_copy(
            src_ref=rows_ref.at[y_at[k], pl.ds(b * BLOCK, BLOCK)],
            dst_ref=out_ref.at[at * blocks + b],
            send_sem=send.at[b, k - 1],
            recv_sem=recv.at[b, k - 1],
            device_id={"mp": y_at[k]},
            device_id_type=MESH,
        )

    for b in range(blocks):
        get(b).wait()
        here = slice(b * BLOCK, (b + 1) * BLOCK)
        ah, al = split(agg[here, :])
        done = mm3(ah, al, wh, wl)
        for m in range(MP):
            rows_ref[m, here, :] = done[:, m * width : (m + 1) * width]
        if b == 0:
            pl.semaphore_wait(barrier, MP - 1)
        for k in (2, 1, 3):
            copy(b, k, me).start()
        out_ref[me * blocks + b] = rows_ref[me, here, :]
    for b in range(blocks):
        for k in range(1, MP):
            copy(b, k, y_from[k]).wait_recv()
            copy(b, k, me).wait_send()


def exchange(agg, dec_out_w):
    dma = pltpu.SemaphoreType.DMA
    vmem = pl.BlockSpec(memory_space=pltpu.VMEM)
    hbm = pl.BlockSpec(memory_space=pltpu.HBM)
    share, hid = agg.shape
    width = dec_out_w.shape[2] // MP
    blocks = share // BLOCK
    return pl.pallas_call(
        exchange_kernel,
        in_specs=[hbm, hbm],
        out_specs=vmem,
        out_shape=jax.ShapeDtypeStruct((MP * blocks, BLOCK, width), F32),
        scratch_shapes=[
            pltpu.VMEM((share, hid), F32),
            pltpu.VMEM(dec_out_w.shape, F32),
            pltpu.VMEM((MP, share, width), F32),
            dma((blocks, MP - 1)),
            dma((blocks, MP - 1)),
            dma((blocks + 1,)),
        ],
        compiler_params=pltpu.CompilerParams(
            collective_id=1, has_side_effects=True, vmem_limit_bytes=62 << 20
        ),
        name="exchange",
    )(agg, dec_out_w)


def finish_kernel(order, grid_hbm, rows_hbm, out_hbm, held, rows_ref, sums, sems, row_sems, out_sems):
    blocks, _, width = rows_hbm.shape
    columns = pl.ds(pl.multiple_of(lax.axis_index("mp") * width, width), width)

    def place(p):
        return pl.ds(pl.multiple_of(order[0, p] * BLOCK, BLOCK), BLOCK)

    def get(p):
        return pltpu.make_async_copy(grid_hbm.at[place(p), columns], held.at[p], sems.at[p])

    def put(p):
        return pltpu.make_async_copy(sums.at[p], out_hbm.at[place(p)], out_sems.at[p])

    def get_rows(p):
        return pltpu.make_async_copy(rows_hbm.at[p], rows_ref.at[p], row_sems.at[p])

    for p in range(blocks):
        get_rows(p).start()
        get(p).start()
    for p in range(blocks):
        get_rows(p).wait()
        get(p).wait()
        sums[p] = held[p] + rows_ref[p]
        put(p).start()
    for p in range(blocks):
        put(p).wait()


def finish(order, grid_latent, rows):
    blocks, _, width = rows.shape
    hbm = pl.BlockSpec(memory_space=pltpu.HBM)
    dma = pltpu.SemaphoreType.DMA
    return pl.pallas_call(
        finish_kernel,
        in_specs=[pl.BlockSpec(memory_space=pltpu.SMEM), hbm, hbm],
        out_specs=hbm,
        out_shape=jax.ShapeDtypeStruct((blocks * BLOCK, width), F32),
        scratch_shapes=[
            pltpu.VMEM(rows.shape, F32),
            pltpu.VMEM(rows.shape, F32),
            pltpu.VMEM(rows.shape, F32),
            dma((blocks,)),
            dma((blocks,)),
            dma((blocks,)),
        ],
        compiler_params=pltpu.CompilerParams(vmem_limit_bytes=62 << 20),
        name="finish",
    )(order, grid_latent, rows)


def decoder_kernel(
    tiles, order, edges_hbm, gcat_hbm, mesh_hbm, agg, edges_ref, gcat, mesh_ref, mcat, sems
):
    rows, hid = agg.shape
    width = mesh_hbm.shape[2]
    blocks = rows // BLOCK
    node = lax.axis_index("nodes")
    nodes = lax.axis_size("nodes")
    me = lax.axis_index("mp")
    first = node * MP * blocks
    fetch_mesh = pltpu.make_async_copy(mesh_hbm, mesh_ref, sems.at[0])
    fetch_mesh.start()
    fetch_edges = pltpu.make_async_copy(edges_hbm, edges_ref, sems.at[1])
    fetch_edges.start()
    fetch_gcat = pltpu.make_async_copy(gcat_hbm, gcat, sems.at[2])
    fetch_gcat.start()
    agg[...] = jnp.zeros_like(agg)
    mine = [order[0, me * blocks + s] for s in range(blocks)]
    fetch_mesh.wait()
    high, low = split(mesh_ref[...].reshape(-1, width))
    mcat[:, :hid] = high
    mcat[:, hid:] = low
    fetch_edges.wait()
    fetch_gcat.wait()

    def body(t, carry):
        block = tiles[1, t] - first
        spot = jnp.int32(-1)
        for s in range(blocks):
            spot = jnp.where(block == mine[s], s, spot)

        @pl.when(spot >= 0)
        def _():
            beside = lax.rem(tiles[0, t] - (node - 1) + nodes, nodes)
            ids = edges_ref[t]
            hot = one_hot_cols(ids[1:2])
            picked = jnp.concatenate([one_hot_cols(ids[0:1]), hot], axis=0)
            here = pl.ds(pl.multiple_of(spot * BLOCK, BLOCK), BLOCK)
            there = pl.ds(pl.multiple_of(beside * BLOCK, BLOCK), BLOCK)
            table = jnp.concatenate([mcat[there, :], gcat[here, :]], axis=0)
            pre = mm_first(picked, table)
            mh, ml = split(silu(pre[:, :hid] + pre[:, hid:]))
            agg[here, :] += mm(hot, mh) + mm(hot, ml)

        return carry

    lax.fori_loop(0, edges_ref.shape[0], body, 0)


def decoder(gdec, mesh_beside, dec_tiles, dec_edges, order):
    share, hid = gdec.shape[0], gdec.shape[1] // 2
    smem = pl.BlockSpec(memory_space=pltpu.SMEM)
    hbm = pl.BlockSpec(memory_space=pltpu.HBM)
    return pl.pallas_call(
        decoder_kernel,
        in_specs=[smem, smem, hbm, hbm, hbm],
        out_specs=pl.BlockSpec(memory_space=pltpu.VMEM),
        out_shape=jax.ShapeDtypeStruct((share, hid), F32),
        scratch_shapes=[
            pltpu.VMEM(dec_edges.shape, jnp.int32),
            pltpu.VMEM(gdec.shape, BF16),
            pltpu.VMEM(mesh_beside.shape, F32),
            pltpu.VMEM((3 * BLOCK, 2 * hid), BF16),
            pltpu.SemaphoreType.DMA((3,)),
        ],
        compiler_params=pltpu.CompilerParams(vmem_limit_bytes=62 << 20),
        name="decoder",
    )(dec_tiles, order, dec_edges, gdec, mesh_beside)


def per_device(
    grid_latent,
    mesh_latent,
    enc_grid_w,
    enc_mesh_w,
    enc_out_w,
    block_gain,
    query_w,
    key_w,
    value_w,
    out_w,
    up_w,
    down_w,
    dec_gain,
    dec_grid_w,
    dec_mesh_w,
    dec_out_w,
    neighbor_blocks,
    enc_tiles,
    enc_edges,
    dec_tiles,
    dec_edges,
):
    arrays = dict(
        enc_grid_w=enc_grid_w,
        mesh_latent=mesh_latent,
        enc_mesh_w=enc_mesh_w,
        enc_edges=enc_edges,
        enc_out_w=enc_out_w,
        block_gain=block_gain[None],
        query_w=query_w,
        key_w=key_w,
        value_w=value_w,
        out_w=out_w,
        up_w=up_w,
        down_w=down_w,
        dec_gain=dec_gain[None],
        dec_grid_w=dec_grid_w,
        dec_mesh_w=dec_mesh_w,
        dec_out_w=dec_out_w,
    )
    order = assign(dec_tiles.T)
    beside, gdec, dec_out_all = mesh_part(
        enc_tiles.T, neighbor_blocks.T, order, grid_latent, arrays
    )
    agg = decoder(gdec, beside, dec_tiles.T, dec_edges, order)
    return finish(order, grid_latent, exchange(agg, dec_out_all))


def solution(mesh):
    in_specs = (
        P("nodes", None),
        P("nodes", None),
        P(None, "mp"),
        P(None, "mp"),
        P("mp", None),
        P(),
        P(None, "mp"),
        P(None, "mp"),
        P(None, "mp"),
        P("mp", None),
        P(None, "mp"),
        P("mp", None),
        P(),
        P(None, "mp"),
        P(None, "mp"),
        P("mp", None),
        P(),
        P("nodes", None),
        P("nodes", None, None),
        P("nodes", None),
        P("nodes", None, None),
    )
    out_specs = P("nodes", "mp")
    return jax.shard_map(
        per_device, mesh=mesh, in_specs=in_specs, out_specs=out_specs, check_vma=False
    )
```

```python
import math

import jax
import jax.numpy as jnp
from jax import lax
from jax.experimental import pallas as pl
from jax.experimental.pallas import tpu as pltpu
from jax.sharding import PartitionSpec as P

HEAD_DIM = 128
BLOCK = 128
FULL = lax.Precision.HIGHEST
F32 = jnp.float32
BF16 = jnp.bfloat16


def product(matrix, weight):
    return jnp.dot(matrix, weight, precision=FULL, preferred_element_type=F32)


def split(x):
    high = x.astype(BF16)
    low = (x - high.astype(F32)).astype(BF16)
    return high, low


def mm(a, b):
    return jnp.dot(a, b, preferred_element_type=F32)


def mm_first(a, b):
    return lax.dot_general(a, b, (((0,), (0,)), ((), ())), preferred_element_type=F32)


def silu(v):
    half = 0.5 * v
    return half + half * jnp.tanh(half)


def one_hot_cols(row):
    sub = lax.broadcasted_iota(jnp.int32, (BLOCK, BLOCK), 0)
    return jnp.where(row == sub, 1.0, 0.0).astype(BF16)


MESH = pl.DeviceIdType.MESH
Z, X, MP = 8, 4, 4
CHIPS = Z * X
CHUNKS = ((0, 72), (72, 56))


def spans(chunk):
    return (1 - Z // 2, Z // 2), (1 - X // 2, X // 2)


def onward(chunk, dz, dx):
    zs, xs = spans(chunk)
    steps = []

    def along_z(start):
        if dz >= 0 and dz + 1 <= zs[1] and (start or dz > 0):
            steps.append((1, 0))
        if dz <= 0 and dz - 1 >= zs[0] and (start or dz < 0):
            steps.append((-1, 0))

    def along_x(start):
        if dx >= 0 and dx + 1 <= xs[1] and (start or dx > 0):
            steps.append((0, 1))
        if dx <= 0 and dx - 1 >= xs[0] and (start or dx < 0):
            steps.append((0, -1))

    if chunk == 0:
        if dx == 0:
            along_z(dz == 0)
            along_x(True)
        else:
            along_x(False)
    else:
        if dz == 0:
            along_x(dx == 0)
            along_z(True)
        else:
            along_z(False)
    return sorted(steps, key=lambda step: not branching(chunk, step))


def arrivals():
    events = []
    for chunk in range(len(CHUNKS)):
        zs, xs = spans(chunk)
        for dz in range(zs[0], zs[1] + 1):
            for dx in range(xs[0], xs[1] + 1):
                if (dz, dx) != (0, 0):
                    first, second = (dz, dx) if chunk == 0 else (dx, dz)
                    order = (abs(dz) + abs(dx), second != 0, abs(second))
                    events.append((order, chunk, dz, dx, slot_of(chunk, dz, dx)))
    return sorted(events)


def branching(chunk, step):
    return (step[0] != 0) == (chunk == 0)


def slot_of(chunk, dz, dx):
    zs, xs = spans(chunk)
    return (dz - zs[0]) * X + dx - xs[0]


def norm_rows(x, gain):
    centre = jnp.mean(x, axis=-1, keepdims=True)
    shifted = x - centre
    spread = jnp.mean(shifted * shifted, axis=-1, keepdims=True)
    return shifted * lax.rsqrt(spread + 1e-05) * gain


def mm3(ah, al, bh, bl):
    return mm(ah, bh) + mm(ah, bl) + mm(al, bh)


FETCHED = (
    "enc_grid_w",
    "mesh_latent",
    "enc_mesh_w",
    "enc_edges",
    "enc_out_w",
    "dec_grid_w",
    "block_gain",
    "key_w",
    "value_w",
    "up_w",
    "down_w",
    "query_w",
    "out_w",
    "dec_mesh_w",
    "dec_out_w",
    "dec_gain",
)


def mesh_kernel(tiles, lists, order, grid_hbm, *refs):
    count = len(FETCHED)
    given = dict(zip(FETCHED, refs[:count]))
    beside, gdec, dec_out_all = refs[count : count + 3]
    rest = refs[count + 3 :]
    held = dict(zip(FETCHED, rest[:count]))
    (
        grid_ref,
        wcat,
        gcat,
        mcat,
        acc,
        agg_all,
        enc_out_all,
        out_all,
        dec_mesh_all,
        dec_grid_all,
        kv,
        partial,
        parts,
        summed,
        att_all,
        scores,
        out_cat,
        dec_cat,
        fetch_sem,
        grid_sem,
        y_send,
        y_recv,
        c_send,
        c_recv,
        link_send,
        link_recv,
        core_send,
        core_recv,
        side_send,
        side_recv,
    ) = rest[count:]
    chunk_rows = 256

    def fetch(name):
        return pltpu.make_async_copy(
            given[name], held[name], fetch_sem.at[FETCHED.index(name)]
        )

    def fetch_rows(i):
        here = pl.ds(pl.multiple_of(i * chunk_rows, chunk_rows), chunk_rows)
        there = pl.ds(i * (chunk_rows // BLOCK), chunk_rows // BLOCK)
        return pltpu.make_async_copy(
            grid_hbm.at[here].reshape(chunk_rows // BLOCK, BLOCK, grid_hbm.shape[1]),
            grid_ref.at[there],
            grid_sem.at[i],
        )

    for name in FETCHED[:3]:
        fetch(name).start()
    for i in range(grid_hbm.shape[0] // chunk_rows):
        fetch_rows(i).start()
    for name in FETCHED[3:]:
        fetch(name).start()

    def got(name):
        fetch(name).wait()
        return held[name][...]

    me = lax.axis_index("mp")
    node = lax.axis_index("nodes")
    nodes = Z * X * 2
    core = lax.rem(node, 2)
    chip = node // 2
    z, x = chip // X, lax.rem(chip, X)
    way = 1 - 2 * core
    z_at = {d: lax.rem(z + way * d + Z, Z) for d in range(-4, 5)}
    x_at = {d: lax.rem(x + way * d + X, X) for d in range(-2, 3)}
    sibling = node + way
    y_at = [lax.rem(me + k, MP) for k in range(MP)]
    y_from = [lax.rem(me + MP - k, MP) for k in range(MP)]
    after, before = lax.rem(node + 1, nodes), lax.rem(node + nodes - 1, nodes)
    beyond = jnp.where(core == 0, before, after)

    def chip_node(dz, dx):
        return (z_at[dz] * X + x_at[dx]) * 2 + core

    barrier = pltpu.get_barrier_semaphore()
    for dz, dx in ((1, 0), (-1, 0), (0, 1), (0, -1)):
        pl.semaphore_signal(
            barrier, inc=1, device_id={"nodes": chip_node(dz, dx)}, device_id_type=MESH
        )
    pl.semaphore_signal(barrier, inc=1, device_id={"nodes": sibling}, device_id_type=MESH)
    pl.semaphore_signal(barrier, inc=1, device_id={"nodes": beyond}, device_id_type=MESH)
    for k in range(1, MP):
        pl.semaphore_signal(barrier, inc=1, device_id={"mp": y_at[k]}, device_id_type=MESH)
    pl.semaphore_wait(barrier, 9)

    def y_copy(item, k, src, dst):
        return pltpu.make_async_remote_copy(
            src_ref=src,
            dst_ref=dst,
            send_sem=y_send.at[item, k - 1],
            recv_sem=y_recv.at[item, k - 1],
            device_id={"mp": y_at[k]},
            device_id_type=MESH,
        )

    def c_copy(item, k, ref):
        return pltpu.make_async_remote_copy(
            src_ref=ref,
            dst_ref=ref,
            send_sem=c_send.at[item, k - 1],
            recv_sem=c_recv.at[item, k - 1],
            device_id={"nodes": sibling},
            device_id_type=MESH,
        )

    weights = {
        0: ("enc_out_w", enc_out_all),
        1: ("dec_grid_w", dec_grid_all),
        2: ("out_w", out_all),
        3: ("dec_mesh_w", dec_mesh_all),
        4: ("dec_out_w", dec_out_all),
    }

    def halves(item):
        half = given[weights[item][0]].shape[0] // 2
        return pl.ds(pl.multiple_of(core * half, half), half), pl.ds(
            pl.multiple_of((1 - core) * half, half), half
        )

    def weight_start(item):
        name, whole = weights[item]
        own = given[name]
        mine, _ = halves(item)
        for k in range(1, MP):
            y_copy(item, k, own.at[mine], whole.at[me, mine]).start()

    def weight_pass_on(item):
        name, whole = weights[item]
        own = given[name]
        mine, _ = halves(item)
        for k in range(1, MP):
            y_copy(item, k, own.at[mine], whole.at[y_from[k], mine]).wait_recv()
            c_copy(item, k, whole.at[y_from[k], mine]).start()

    def weight_finish(item):
        name, whole = weights[item]
        own = given[name]
        mine, other = halves(item)
        whole[me] = got(name)
        for k in range(1, MP):
            c_copy(item, k, whole.at[y_from[k], other]).wait_recv()
        for k in range(1, MP):
            y_copy(item, k, own.at[mine], whole.at[me, mine]).wait_send()
            c_copy(item, k, whole.at[y_from[k], mine]).wait_send()

    weight_start(0)

    rows, hid = grid_hbm.shape[0], given["enc_grid_w"].shape[1]
    blocks = rows // BLOCK
    enc_edges = held["enc_edges"]
    slots = enc_edges.shape[0]
    high, low = split(got("enc_grid_w"))
    wcat[:, :hid] = high
    wcat[:, hid:] = low
    high, low = split(product(got("mesh_latent"), got("enc_mesh_w")))
    mcat[:, :hid] = high
    mcat[:, hid:] = low
    acc[...] = jnp.zeros_like(acc)

    def project(i, carry):
        fetch_rows(i).wait()
        there = pl.ds(i * (chunk_rows // BLOCK), chunk_rows // BLOCK)
        xh, xl = split(grid_ref[there].reshape(chunk_rows, -1))
        both = mm(xh, wcat[...]) + mm(xl, wcat[...])
        high, low = split(both[:, :hid] + both[:, hid:])
        for j in range(chunk_rows // BLOCK):
            part = slice(j * BLOCK, (j + 1) * BLOCK)
            gcat[i * (chunk_rows // BLOCK) + j, :, :hid] = high[part]
            gcat[i * (chunk_rows // BLOCK) + j, :, hid:] = low[part]
        return carry

    lax.fori_loop(0, rows // chunk_rows, project, 0)
    first = node * blocks
    group = 8

    def edges(i, carry):
        hots, messages = [], []
        for k in range(group):
            t = i * group + k
            tile = tiles[0, t]
            live = tile >= 0
            block = jnp.clip(tile - first, 0, blocks - 1)
            ids = enc_edges[t]
            target = one_hot_cols(jnp.where(live, ids[1:2], -1))
            picked = jnp.concatenate([one_hot_cols(ids[0:1]), target], axis=0)
            table = jnp.concatenate([gcat[block], mcat[...]], axis=0)
            pre = mm_first(picked, table)
            mh, ml = split(silu(pre[:, :hid] + pre[:, hid:]))
            messages.append(jnp.concatenate([mh, ml], axis=1))
            hots.append(target)
        acc[...] += mm(jnp.concatenate(hots, axis=1), jnp.concatenate(messages, axis=0))
        return carry

    half_way = slots // group // 2
    fetch("enc_edges").wait()
    lax.fori_loop(0, half_way, edges, 0)
    weight_pass_on(0)
    lax.fori_loop(half_way, slots // group, edges, 0)
    agg_all[me] = acc[:, :hid] + acc[:, hid:]
    for k in range(1, MP):
        y_copy(5, k, agg_all.at[me], agg_all.at[me]).start()
    weight_finish(0)
    for k in range(1, MP):
        y_copy(5, k, agg_all.at[me], agg_all.at[y_from[k]]).wait_recv()
    agg = jnp.concatenate([agg_all[m] for m in range(MP)], axis=1)
    width = grid_hbm.shape[1]
    mesh_one = held["mesh_latent"][...] + product(agg, enc_out_all[...].reshape(width, width))
    normed = norm_rows(mesh_one, got("block_gain"))
    own_kv = product(normed, jnp.concatenate([got("key_w"), got("value_w")], axis=1))
    here = core * CHIPS + chip
    kv[here] = own_kv

    def link_copy(chunk, pos, slot, step):
        start, size = CHUNKS[chunk]
        piece = kv.at[pos, pl.ds(start, size)]
        return pltpu.make_async_remote_copy(
            src_ref=piece,
            dst_ref=piece,
            send_sem=link_send,
            recv_sem=link_recv.at[chunk, slot],
            device_id={"nodes": chip_node(*step)},
            device_id_type=MESH,
        )

    def core_copy(ref):
        return pltpu.make_async_remote_copy(
            src_ref=ref,
            dst_ref=ref,
            send_sem=core_send,
            recv_sem=core_recv,
            device_id={"nodes": sibling},
            device_id_type=MESH,
        )

    starts = [(chunk, step) for chunk in range(len(CHUNKS)) for step in onward(chunk, 0, 0)]
    for chunk, step in sorted(starts, key=lambda s: not branching(*s)):
        link_copy(chunk, here, slot_of(chunk, *step), step).start()
    core_copy(kv.at[here]).start()
    weight_start(1)

    def arrive(event):
        _, chunk, dz, dx, slot = event
        pos = core * CHIPS + z_at[-dz] * X + x_at[-dx]
        start, size = CHUNKS[chunk]
        link_copy(chunk, pos, slot, (1, 0)).wait_recv()
        for step in onward(chunk, dz, dx):
            link_copy(
                chunk, pos, slot_of(chunk, dz + step[0], dx + step[1]), step
            ).start()
        core_copy(kv.at[pos, pl.ds(start, size)]).start()

    nh, nl = split(normed)
    uh, ul = split(got("up_w"))
    hidden = silu(mm3(nh, nl, uh, ul))
    queue = arrivals()
    near = [e for e in queue if e[0][0] == 1]
    rest = [e for e in queue if e[0][0] > 1]
    assert gdec.shape[0] == 4 * BLOCK
    for event in near:
        arrive(event)
    hh, hl = split(hidden)
    dh, dl = split(got("down_w"))
    partial[...] = mm3(hh, hl, dh, dl)
    share = BLOCK // MP

    def share_of(m):
        return pl.ds(pl.multiple_of(m * share, share), share)

    for k in range(1, MP):
        y_copy(6, k, partial.at[share_of(y_at[k])], parts.at[me]).start()
    for item in (2, 3, 4):
        weight_start(item)
    weight_pass_on(1)
    rest_count = len(rest)
    third = rest_count // 4
    for event in rest[:third]:
        arrive(event)
    weight_finish(1)
    gh, gl = split(jnp.concatenate([dec_grid_all[m] for m in range(MP)], axis=1))

    def grid_decode(b):
        block = jnp.clip(order[0, me * MP + b], 0, blocks - 1)
        xh, xl = split(grid_ref[block])
        high, low = split(mm3(xh, xl, gh, gl))
        gdec[b * BLOCK : (b + 1) * BLOCK, :width] = high
        gdec[b * BLOCK : (b + 1) * BLOCK, width:] = low

    grid_decode(0)
    for k in range(1, MP):
        y_copy(6, k, partial.at[share_of(y_at[k])], parts.at[y_from[k]]).wait_recv()
    summed[share_of(me), :] = partial[share_of(me), :] + (
        parts[y_from[1]] + parts[y_from[2]] + parts[y_from[3]]
    )
    for k in range(1, MP):
        y_copy(7, k, summed.at[share_of(me)], summed.at[share_of(me)]).start()
    queries = product(normed, got("query_w")) * (1.0 / math.sqrt(HEAD_DIM))
    for event in rest[third : 2 * third]:
        arrive(event)
    grid_decode(1)
    weight_pass_on(2)
    for event in rest[2 * third : 3 * third]:
        arrive(event)
    grid_decode(2)
    weight_pass_on(3)
    for event in rest[3 * third :]:
        arrive(event)
    weight_pass_on(4)
    grid_decode(3)
    for k in range(1, MP):
        y_copy(7, k, summed.at[share_of(me)], summed.at[share_of(y_from[k])]).wait_recv()
    mesh_mid = mesh_one + summed[...]
    for item, whole in ((2, out_cat), (3, dec_cat)):
        weight_finish(item)
        if item == 2:
            high, low = split(out_all[...].reshape(width, width))
        else:
            high, low = split(jnp.concatenate([dec_mesh_all[m] for m in range(MP)], axis=1))
        whole[:, :width] = high
        whole[:, width:] = low
    core_copy(kv.at[pl.ds((1 - core) * CHIPS, CHIPS)]).wait_recv()

    count = lists.shape[0]
    top = jnp.full((BLOCK, 1), -jnp.inf, F32)
    spots = []
    for j in range(count):
        block = lists[j, node]
        spot = jnp.bitwise_and(block, 1) * CHIPS + jnp.right_shift(block, 1)
        spots.append(spot)
        logit = lax.dot_general(
            queries,
            kv[spot][:, :HEAD_DIM],
            (((1,), (1,)), ((), ())),
            precision=FULL,
            preferred_element_type=F32,
        )
        scores[:, j * BLOCK : (j + 1) * BLOCK] = logit
        top = jnp.maximum(top, jnp.max(logit, axis=-1, keepdims=True))
    weight = jnp.exp(scores[...] - top)
    total = jnp.sum(weight, axis=-1, keepdims=True)
    values = jnp.concatenate([kv[spot][:, HEAD_DIM:] for spot in spots], axis=0)
    wh, wl = split(weight)
    vh, vl = split(values)
    att_all[me] = mm3(wh, wl, vh, vl) / total
    for k in range(1, MP):
        y_copy(8, k, att_all.at[me], att_all.at[me]).start()
    for k in range(1, MP):
        y_copy(8, k, att_all.at[me], att_all.at[y_from[k]]).wait_recv()
    attended = jnp.concatenate([att_all[m] for m in range(MP)], axis=1)
    mesh_two = mesh_mid + mm3(*split(attended), out_cat[:, :width], out_cat[:, width:])
    normed_two = norm_rows(mesh_two, got("dec_gain"))
    beside[1] = mm3(*split(normed_two), dec_cat[:, :width], dec_cat[:, width:])

    def side_copy(way, slot, target):
        return pltpu.make_async_remote_copy(
            src_ref=beside.at[1],
            dst_ref=beside.at[slot],
            send_sem=side_send.at[way],
            recv_sem=side_recv.at[way],
            device_id={"nodes": target},
            device_id_type=MESH,
        )

    side_copy(0, 0, after).start()
    side_copy(1, 2, before).start()
    weight_finish(4)
    core_copy(kv.at[pl.ds(core * CHIPS, CHIPS)]).wait_send()
    link_copy_all = pltpu.make_async_remote_copy(
        src_ref=kv.at[pl.ds(0, CHIPS - 1)],
        dst_ref=kv.at[pl.ds(0, CHIPS - 1)],
        send_sem=link_send,
        recv_sem=link_recv.at[0, 0],
        device_id={"nodes": sibling},
        device_id_type=MESH,
    )
    link_copy_all.wait_send()
    for item, ref in ((5, agg_all.at[me]), (8, att_all.at[me])):
        for k in range(1, MP):
            y_copy(item, k, ref, ref).wait_send()
    for item in (6, 7):
        for k in range(1, MP):
            ref = summed.at[share_of(me)]
            y_copy(item, k, ref, ref).wait_send()
    side_copy(0, 0, after).wait()
    side_copy(1, 2, before).wait()


def mesh_part(tiles, lists, order, grid_latent, arrays):
    rows, width = grid_latent.shape
    nodes = arrays["mesh_latent"].shape[0]
    hid = arrays["enc_grid_w"].shape[1]
    vmem = pl.BlockSpec(memory_space=pltpu.VMEM)
    smem = pl.BlockSpec(memory_space=pltpu.SMEM)
    hbm = pl.BlockSpec(memory_space=pltpu.HBM)
    dma = pltpu.SemaphoreType.DMA
    listed = lists.shape[0]
    operands = [arrays[name] for name in FETCHED]
    return pl.pallas_call(
        mesh_kernel,
        in_specs=[smem, smem, smem, hbm] + [hbm] * len(operands),
        out_specs=[vmem] * 3,
        out_shape=[
            jax.ShapeDtypeStruct((3, nodes, width), F32),
            jax.ShapeDtypeStruct((rows // MP, 2 * width), BF16),
            jax.ShapeDtypeStruct((MP, hid, width), F32),
        ],
        scratch_shapes=[pltpu.VMEM(array.shape, array.dtype) for array in operands]
        + [
            pltpu.VMEM((rows // BLOCK, BLOCK, width), F32),
            pltpu.VMEM((width, 2 * hid), BF16),
            pltpu.VMEM((rows // BLOCK, BLOCK, 2 * hid), BF16),
            pltpu.VMEM((nodes, 2 * hid), BF16),
            pltpu.VMEM((nodes, 2 * hid), F32),
            pltpu.VMEM((MP, nodes, hid), F32),
            pltpu.VMEM((MP, hid, width), F32),
            pltpu.VMEM((MP, hid, width), F32),
            pltpu.VMEM((MP, width, hid), F32),
            pltpu.VMEM((MP, width, hid), F32),
            pltpu.VMEM((2 * CHIPS, nodes, 2 * HEAD_DIM), F32),
            pltpu.VMEM((nodes, width), F32),
            pltpu.VMEM((MP, nodes // MP, width), F32),
            pltpu.VMEM((nodes, width), F32),
            pltpu.VMEM((MP, nodes, HEAD_DIM), F32),
            pltpu.VMEM((nodes, listed * BLOCK), F32),
            pltpu.VMEM((width, 2 * width), BF16),
            pltpu.VMEM((width, 2 * width), BF16),
            dma((len(operands),)),
            dma((rows // 256,)),
            dma((9, MP - 1)),
            dma((9, MP - 1)),
            dma((5, MP - 1)),
            dma((5, MP - 1)),
            dma(()),
            dma((len(CHUNKS), CHIPS)),
            dma(()),
            dma(()),
            dma((2,)),
            dma((2,)),
        ],
        compiler_params=pltpu.CompilerParams(
            collective_id=0, has_side_effects=True, vmem_limit_bytes=62 << 20
        ),
        name="mesh_part",
    )(tiles, lists, order, grid_latent, *operands)


def assign_kernel(tiles_ref, order_ref):
    blocks = MP * MP
    width = tiles_ref.shape[1]
    first = lax.axis_index("nodes") * blocks
    ids = tiles_ref[1:2, :] - first
    block = lax.broadcasted_iota(jnp.int32, (blocks, width), 0)
    tally = jnp.sum(jnp.where(ids == block, 1.0, 0.0), axis=1, keepdims=True)
    wide = jnp.broadcast_to(tally, (blocks, BLOCK))
    across = jnp.concatenate([wide] * (BLOCK // blocks), axis=0).T[:blocks, :blocks]
    down = wide[:, :blocks]
    i = lax.broadcasted_iota(jnp.int32, (blocks, blocks), 0)
    j = lax.broadcasted_iota(jnp.int32, (blocks, blocks), 1)
    ahead = jnp.logical_or(across > down, jnp.logical_and(across == down, j < i))
    rank = jnp.sum(jnp.where(ahead, 1.0, 0.0), axis=1, keepdims=True).astype(jnp.int32)
    device, turn = j // MP, lax.rem(j, MP)
    dealt = jnp.where(lax.rem(turn, 2) == 0, device, MP - 1 - device) + turn * MP
    chosen = jnp.where(rank == dealt, i.astype(F32), 0.0)
    order_ref[...] = jnp.sum(chosen, axis=0, keepdims=True).astype(jnp.int32)


def assign(dec_tiles):
    vmem = pl.BlockSpec(memory_space=pltpu.VMEM)
    return pl.pallas_call(
        assign_kernel,
        in_specs=[vmem],
        out_specs=vmem,
        out_shape=jax.ShapeDtypeStruct((1, MP * MP), jnp.int32),
        name="assign",
    )(dec_tiles)


def exchange_kernel(agg_hbm, wo_hbm, out_ref, agg, wo_ref, rows_ref, send, recv, fetch):
    me = lax.axis_index("mp")
    share, hid = agg_hbm.shape
    width = wo_hbm.shape[2] // MP
    blocks = share // BLOCK
    y_at = [lax.rem(me + k, MP) for k in range(MP)]
    y_from = [lax.rem(me + MP - k, MP) for k in range(MP)]

    def get(b):
        here = pl.ds(b * BLOCK, BLOCK)
        return pltpu.make_async_copy(agg_hbm.at[here], agg.at[here], fetch.at[b])

    get_wo = pltpu.make_async_copy(wo_hbm, wo_ref, fetch.at[blocks])
    get_wo.start()
    for b in range(blocks):
        get(b).start()
    barrier = pltpu.get_barrier_semaphore()
    for k in range(1, MP):
        pl.semaphore_signal(barrier, inc=1, device_id={"mp": y_at[k]}, device_id_type=MESH)
    get_wo.wait()
    wh, wl = split(wo_ref[...].reshape(hid, MP * width))

    def copy(b, k, at):
        return pltpu.make_async_remote_copy(
            src_ref=rows_ref.at[y_at[k], pl.ds(b * BLOCK, BLOCK)],
            dst_ref=out_ref.at[at * blocks + b],
            send_sem=send.at[b, k - 1],
            recv_sem=recv.at[b, k - 1],
            device_id={"mp": y_at[k]},
            device_id_type=MESH,
        )

    for b in range(blocks):
        get(b).wait()
        here = slice(b * BLOCK, (b + 1) * BLOCK)
        ah, al = split(agg[here, :])
        done = mm3(ah, al, wh, wl)
        for m in range(MP):
            rows_ref[m, here, :] = done[:, m * width : (m + 1) * width]
        if b == 0:
            pl.semaphore_wait(barrier, MP - 1)
        for k in (2, 1, 3):
            copy(b, k, me).start()
        out_ref[me * blocks + b] = rows_ref[me, here, :]
    for b in range(blocks):
        for k in range(1, MP):
            copy(b, k, y_from[k]).wait_recv()
            copy(b, k, me).wait_send()


def exchange(agg, dec_out_w):
    dma = pltpu.SemaphoreType.DMA
    vmem = pl.BlockSpec(memory_space=pltpu.VMEM)
    hbm = pl.BlockSpec(memory_space=pltpu.HBM)
    share, hid = agg.shape
    width = dec_out_w.shape[2] // MP
    blocks = share // BLOCK
    return pl.pallas_call(
        exchange_kernel,
        in_specs=[hbm, hbm],
        out_specs=vmem,
        out_shape=jax.ShapeDtypeStruct((MP * blocks, BLOCK, width), F32),
        scratch_shapes=[
            pltpu.VMEM((share, hid), F32),
            pltpu.VMEM(dec_out_w.shape, F32),
            pltpu.VMEM((MP, share, width), F32),
            dma((blocks, MP - 1)),
            dma((blocks, MP - 1)),
            dma((blocks + 1,)),
        ],
        compiler_params=pltpu.CompilerParams(
            collective_id=1, has_side_effects=True, vmem_limit_bytes=62 << 20
        ),
        name="exchange",
    )(agg, dec_out_w)


def finish_kernel(order, grid_hbm, rows_hbm, out_hbm, held, rows_ref, sums, sems, row_sems, out_sems):
    blocks, _, width = rows_hbm.shape
    columns = pl.ds(pl.multiple_of(lax.axis_index("mp") * width, width), width)

    def place(p):
        return pl.ds(pl.multiple_of(order[0, p] * BLOCK, BLOCK), BLOCK)

    def get(p):
        return pltpu.make_async_copy(grid_hbm.at[place(p), columns], held.at[p], sems.at[p])

    def put(p):
        return pltpu.make_async_copy(sums.at[p], out_hbm.at[place(p)], out_sems.at[p])

    def get_rows(p):
        return pltpu.make_async_copy(rows_hbm.at[p], rows_ref.at[p], row_sems.at[p])

    for p in range(blocks):
        get_rows(p).start()
        get(p).start()
    for p in range(blocks):
        get_rows(p).wait()
        get(p).wait()
        sums[p] = held[p] + rows_ref[p]
        put(p).start()
    for p in range(blocks):
        put(p).wait()


def finish(order, grid_latent, rows):
    blocks, _, width = rows.shape
    hbm = pl.BlockSpec(memory_space=pltpu.HBM)
    dma = pltpu.SemaphoreType.DMA
    return pl.pallas_call(
        finish_kernel,
        in_specs=[pl.BlockSpec(memory_space=pltpu.SMEM), hbm, hbm],
        out_specs=hbm,
        out_shape=jax.ShapeDtypeStruct((blocks * BLOCK, width), F32),
        scratch_shapes=[
            pltpu.VMEM(rows.shape, F32),
            pltpu.VMEM(rows.shape, F32),
            pltpu.VMEM(rows.shape, F32),
            dma((blocks,)),
            dma((blocks,)),
            dma((blocks,)),
        ],
        compiler_params=pltpu.CompilerParams(vmem_limit_bytes=62 << 20),
        name="finish",
    )(order, grid_latent, rows)


def decoder_kernel(
    tiles, order, edges_hbm, gcat_hbm, mesh_hbm, agg, edges_ref, gcat, mesh_ref, mcat, todo, sems
):
    rows, hid = agg.shape
    width = mesh_hbm.shape[2]
    blocks = rows // BLOCK
    node = lax.axis_index("nodes")
    nodes = lax.axis_size("nodes")
    me = lax.axis_index("mp")
    first = node * MP * blocks
    group = 2
    fetch_mesh = pltpu.make_async_copy(mesh_hbm, mesh_ref, sems.at[0])
    fetch_mesh.start()
    fetch_edges = pltpu.make_async_copy(edges_hbm, edges_ref, sems.at[1])
    fetch_edges.start()
    fetch_gcat = pltpu.make_async_copy(gcat_hbm, gcat, sems.at[2])
    fetch_gcat.start()
    agg[...] = jnp.zeros_like(agg)
    mine = [order[0, me * blocks + s] for s in range(blocks)]
    fetch_mesh.wait()
    high, low = split(mesh_ref[...].reshape(-1, width))
    mcat[:, :hid] = high
    mcat[:, hid:] = low
    fetch_edges.wait()
    fetch_gcat.wait()

    def pick(t, found):
        block = tiles[1, t] - first
        spot = jnp.int32(-1)
        for s in range(blocks):
            spot = jnp.where(block == mine[s], s, spot)
        todo[0, found] = t
        todo[1, found] = spot
        return found + jnp.where(spot >= 0, 1, 0)

    found = lax.fori_loop(0, edges_ref.shape[0], pick, jnp.int32(0))
    for k in range(group):
        todo[0, found + k] = 0
        todo[1, found + k] = -1

    def body(i, carry):
        for k in range(group):
            t, spot = todo[0, i * group + k], todo[1, i * group + k]
            live = spot >= 0
            beside = lax.rem(tiles[0, t] - (node - 1) + nodes, nodes)
            ids = edges_ref[t]
            hot = one_hot_cols(jnp.where(live, ids[1:2], -1))
            picked = jnp.concatenate([one_hot_cols(ids[0:1]), hot], axis=0)
            here = pl.ds(pl.multiple_of(jnp.maximum(spot, 0) * BLOCK, BLOCK), BLOCK)
            there = pl.ds(pl.multiple_of(beside * BLOCK, BLOCK), BLOCK)
            table = jnp.concatenate([mcat[there, :], gcat[here, :]], axis=0)
            pre = mm_first(picked, table)
            mh, ml = split(silu(pre[:, :hid] + pre[:, hid:]))
            agg[here, :] += mm(hot, mh) + mm(hot, ml)
        return carry

    lax.fori_loop(0, (found + group - 1) // group, body, 0)


def decoder(gdec, mesh_beside, dec_tiles, dec_edges, order):
    share, hid = gdec.shape[0], gdec.shape[1] // 2
    smem = pl.BlockSpec(memory_space=pltpu.SMEM)
    hbm = pl.BlockSpec(memory_space=pltpu.HBM)
    return pl.pallas_call(
        decoder_kernel,
        in_specs=[smem, smem, hbm, hbm, hbm],
        out_specs=pl.BlockSpec(memory_space=pltpu.VMEM),
        out_shape=jax.ShapeDtypeStruct((share, hid), F32),
        scratch_shapes=[
            pltpu.VMEM(dec_edges.shape, jnp.int32),
            pltpu.VMEM(gdec.shape, BF16),
            pltpu.VMEM(mesh_beside.shape, F32),
            pltpu.VMEM((3 * BLOCK, 2 * hid), BF16),
            pltpu.SMEM((2, dec_edges.shape[0] + 8), jnp.int32),
            pltpu.SemaphoreType.DMA((3,)),
        ],
        compiler_params=pltpu.CompilerParams(vmem_limit_bytes=62 << 20),
        name="decoder",
    )(dec_tiles, order, dec_edges, gdec, mesh_beside)


def per_device(
    grid_latent,
    mesh_latent,
    enc_grid_w,
    enc_mesh_w,
    enc_out_w,
    block_gain,
    query_w,
    key_w,
    value_w,
    out_w,
    up_w,
    down_w,
    dec_gain,
    dec_grid_w,
    dec_mesh_w,
    dec_out_w,
    neighbor_blocks,
    enc_tiles,
    enc_edges,
    dec_tiles,
    dec_edges,
):
    arrays = dict(
        enc_grid_w=enc_grid_w,
        mesh_latent=mesh_latent,
        enc_mesh_w=enc_mesh_w,
        enc_edges=enc_edges,
        enc_out_w=enc_out_w,
        block_gain=block_gain[None],
        query_w=query_w,
        key_w=key_w,
        value_w=value_w,
        out_w=out_w,
        up_w=up_w,
        down_w=down_w,
        dec_gain=dec_gain[None],
        dec_grid_w=dec_grid_w,
        dec_mesh_w=dec_mesh_w,
        dec_out_w=dec_out_w,
    )
    order = assign(dec_tiles.T)
    beside, gdec, dec_out_all = mesh_part(
        enc_tiles.T, neighbor_blocks.T, order, grid_latent, arrays
    )
    agg = decoder(gdec, beside, dec_tiles.T, dec_edges, order)
    return finish(order, grid_latent, exchange(agg, dec_out_all))


def solution(mesh):
    in_specs = (
        P("nodes", None),
        P("nodes", None),
        P(None, "mp"),
        P(None, "mp"),
        P("mp", None),
        P(),
        P(None, "mp"),
        P(None, "mp"),
        P(None, "mp"),
        P("mp", None),
        P(None, "mp"),
        P("mp", None),
        P(),
        P(None, "mp"),
        P(None, "mp"),
        P("mp", None),
        P(),
        P("nodes", None),
        P("nodes", None, None),
        P("nodes", None),
        P("nodes", None, None),
    )
    out_specs = P("nodes", "mp")
    return jax.shard_map(
        per_device, mesh=mesh, in_specs=in_specs, out_specs=out_specs, check_vma=False
    )
```

```python
import math

import jax
import jax.numpy as jnp
from jax import lax
from jax.experimental import pallas as pl
from jax.experimental.pallas import tpu as pltpu
from jax.sharding import PartitionSpec as P

HEAD_DIM = 128
BLOCK = 128
FULL = lax.Precision.HIGHEST
F32 = jnp.float32
BF16 = jnp.bfloat16


def product(matrix, weight):
    return jnp.dot(matrix, weight, precision=FULL, preferred_element_type=F32)


def split(x):
    high = x.astype(BF16)
    low = (x - high.astype(F32)).astype(BF16)
    return high, low


def mm(a, b):
    return jnp.dot(a, b, preferred_element_type=F32)


def mm_first(a, b):
    return lax.dot_general(a, b, (((0,), (0,)), ((), ())), preferred_element_type=F32)


def silu(v):
    half = 0.5 * v
    return half + half * jnp.tanh(half)


def one_hot_cols(row):
    sub = lax.broadcasted_iota(jnp.int32, (BLOCK, BLOCK), 0)
    return jnp.where(row == sub, 1.0, 0.0).astype(BF16)


MESH = pl.DeviceIdType.MESH
Z, X, MP = 8, 4, 4
CHIPS = Z * X
CHUNKS = ((0, 72), (72, 56))


def spans(chunk):
    return (1 - Z // 2, Z // 2), (1 - X // 2, X // 2)


def onward(chunk, dz, dx):
    zs, xs = spans(chunk)
    steps = []

    def along_z(start):
        if dz >= 0 and dz + 1 <= zs[1] and (start or dz > 0):
            steps.append((1, 0))
        if dz <= 0 and dz - 1 >= zs[0] and (start or dz < 0):
            steps.append((-1, 0))

    def along_x(start):
        if dx >= 0 and dx + 1 <= xs[1] and (start or dx > 0):
            steps.append((0, 1))
        if dx <= 0 and dx - 1 >= xs[0] and (start or dx < 0):
            steps.append((0, -1))

    if chunk == 0:
        if dx == 0:
            along_z(dz == 0)
            along_x(True)
        else:
            along_x(False)
    else:
        if dz == 0:
            along_x(dx == 0)
            along_z(True)
        else:
            along_z(False)
    return sorted(steps, key=lambda step: not branching(chunk, step))


def arrivals():
    events = []
    for chunk in range(len(CHUNKS)):
        zs, xs = spans(chunk)
        for dz in range(zs[0], zs[1] + 1):
            for dx in range(xs[0], xs[1] + 1):
                if (dz, dx) != (0, 0):
                    first, second = (dz, dx) if chunk == 0 else (dx, dz)
                    order = (abs(dz) + abs(dx), second != 0, abs(second))
                    events.append((order, chunk, dz, dx, slot_of(chunk, dz, dx)))
    return sorted(events)


def branching(chunk, step):
    return (step[0] != 0) == (chunk == 0)


def slot_of(chunk, dz, dx):
    zs, xs = spans(chunk)
    return (dz - zs[0]) * X + dx - xs[0]


def norm_rows(x, gain):
    centre = jnp.mean(x, axis=-1, keepdims=True)
    shifted = x - centre
    spread = jnp.mean(shifted * shifted, axis=-1, keepdims=True)
    return shifted * lax.rsqrt(spread + 1e-05) * gain


def mm3(ah, al, bh, bl):
    return mm(ah, bh) + mm(ah, bl) + mm(al, bh)


FETCHED = (
    "enc_grid_w",
    "mesh_latent",
    "enc_mesh_w",
    "enc_edges",
    "enc_out_w",
    "dec_grid_w",
    "block_gain",
    "key_w",
    "value_w",
    "up_w",
    "down_w",
    "query_w",
    "out_w",
    "dec_mesh_w",
    "dec_out_w",
    "dec_gain",
)


def mesh_kernel(tiles, lists, order, grid_hbm, *refs):
    count = len(FETCHED)
    given = dict(zip(FETCHED, refs[:count]))
    beside, gdec, dec_out_all = refs[count : count + 3]
    rest = refs[count + 3 :]
    held = dict(zip(FETCHED, rest[:count]))
    (
        grid_ref,
        wcat,
        gcat,
        mcat,
        acc,
        agg_all,
        enc_out_all,
        out_all,
        dec_mesh_all,
        dec_grid_all,
        kv,
        partial,
        parts,
        summed,
        att_all,
        scores,
        out_cat,
        dec_cat,
        fetch_sem,
        grid_sem,
        y_send,
        y_recv,
        c_send,
        c_recv,
        link_send,
        link_recv,
        core_send,
        core_recv,
        side_send,
        side_recv,
    ) = rest[count:]
    chunk_rows = 256

    def fetch(name):
        return pltpu.make_async_copy(
            given[name], held[name], fetch_sem.at[FETCHED.index(name)]
        )

    def fetch_rows(i):
        here = pl.ds(pl.multiple_of(i * chunk_rows, chunk_rows), chunk_rows)
        there = pl.ds(i * (chunk_rows // BLOCK), chunk_rows // BLOCK)
        return pltpu.make_async_copy(
            grid_hbm.at[here].reshape(chunk_rows // BLOCK, BLOCK, grid_hbm.shape[1]),
            grid_ref.at[there],
            grid_sem.at[i],
        )

    for name in FETCHED[:3]:
        fetch(name).start()
    for i in range(grid_hbm.shape[0] // chunk_rows):
        fetch_rows(i).start()
    for name in FETCHED[3:]:
        fetch(name).start()

    def got(name):
        fetch(name).wait()
        return held[name][...]

    me = lax.axis_index("mp")
    node = lax.axis_index("nodes")
    nodes = Z * X * 2
    core = lax.rem(node, 2)
    chip = node // 2
    z, x = chip // X, lax.rem(chip, X)
    way = 1 - 2 * core
    z_at = {d: lax.rem(z + way * d + Z, Z) for d in range(-4, 5)}
    x_at = {d: lax.rem(x + way * d + X, X) for d in range(-2, 3)}
    sibling = node + way
    y_at = [lax.rem(me + k, MP) for k in range(MP)]
    y_from = [lax.rem(me + MP - k, MP) for k in range(MP)]
    after, before = lax.rem(node + 1, nodes), lax.rem(node + nodes - 1, nodes)
    beyond = jnp.where(core == 0, before, after)

    def chip_node(dz, dx):
        return (z_at[dz] * X + x_at[dx]) * 2 + core

    barrier = pltpu.get_barrier_semaphore()
    for dz, dx in ((1, 0), (-1, 0), (0, 1), (0, -1)):
        pl.semaphore_signal(
            barrier, inc=1, device_id={"nodes": chip_node(dz, dx)}, device_id_type=MESH
        )
    pl.semaphore_signal(barrier, inc=1, device_id={"nodes": sibling}, device_id_type=MESH)
    pl.semaphore_signal(barrier, inc=1, device_id={"nodes": beyond}, device_id_type=MESH)
    for k in range(1, MP):
        pl.semaphore_signal(barrier, inc=1, device_id={"mp": y_at[k]}, device_id_type=MESH)
    pl.semaphore_wait(barrier, 9)

    def y_copy(item, k, src, dst):
        return pltpu.make_async_remote_copy(
            src_ref=src,
            dst_ref=dst,
            send_sem=y_send.at[item, k - 1],
            recv_sem=y_recv.at[item, k - 1],
            device_id={"mp": y_at[k]},
            device_id_type=MESH,
        )

    def c_copy(item, k, ref):
        return pltpu.make_async_remote_copy(
            src_ref=ref,
            dst_ref=ref,
            send_sem=c_send.at[item, k - 1],
            recv_sem=c_recv.at[item, k - 1],
            device_id={"nodes": sibling},
            device_id_type=MESH,
        )

    weights = {
        0: ("enc_out_w", enc_out_all),
        1: ("dec_grid_w", dec_grid_all),
        2: ("out_w", out_all),
        3: ("dec_mesh_w", dec_mesh_all),
        4: ("dec_out_w", dec_out_all),
    }

    def halves(item):
        half = given[weights[item][0]].shape[0] // 2
        return pl.ds(pl.multiple_of(core * half, half), half), pl.ds(
            pl.multiple_of((1 - core) * half, half), half
        )

    def weight_start(item):
        name, whole = weights[item]
        own = given[name]
        mine, _ = halves(item)
        for k in range(1, MP):
            y_copy(item, k, own.at[mine], whole.at[me, mine]).start()

    def weight_pass_on(item):
        name, whole = weights[item]
        own = given[name]
        mine, _ = halves(item)
        for k in range(1, MP):
            y_copy(item, k, own.at[mine], whole.at[y_from[k], mine]).wait_recv()
            c_copy(item, k, whole.at[y_from[k], mine]).start()

    def weight_finish(item):
        name, whole = weights[item]
        own = given[name]
        mine, other = halves(item)
        whole[me] = got(name)
        for k in range(1, MP):
            c_copy(item, k, whole.at[y_from[k], other]).wait_recv()
        for k in range(1, MP):
            y_copy(item, k, own.at[mine], whole.at[me, mine]).wait_send()
            c_copy(item, k, whole.at[y_from[k], mine]).wait_send()

    weight_start(0)

    rows, hid = grid_hbm.shape[0], given["enc_grid_w"].shape[1]
    blocks = rows // BLOCK
    enc_edges = held["enc_edges"]
    slots = enc_edges.shape[0]
    high, low = split(got("enc_grid_w"))
    wcat[:, :hid] = high
    wcat[:, hid:] = low
    high, low = split(product(got("mesh_latent"), got("enc_mesh_w")))
    mcat[:, :hid] = high
    mcat[:, hid:] = low
    acc[...] = jnp.zeros_like(acc)

    def project(i, carry):
        fetch_rows(i).wait()
        there = pl.ds(i * (chunk_rows // BLOCK), chunk_rows // BLOCK)
        xh, xl = split(grid_ref[there].reshape(chunk_rows, -1))
        both = mm(xh, wcat[...]) + mm(xl, wcat[...])
        high, low = split(both[:, :hid] + both[:, hid:])
        for j in range(chunk_rows // BLOCK):
            part = slice(j * BLOCK, (j + 1) * BLOCK)
            gcat[i * (chunk_rows // BLOCK) + j, :, :hid] = high[part]
            gcat[i * (chunk_rows // BLOCK) + j, :, hid:] = low[part]
        return carry

    lax.fori_loop(0, rows // chunk_rows, project, 0)
    first = node * blocks
    group = 8

    def edges(i, carry):
        hots, messages = [], []
        for k in range(group):
            t = i * group + k
            tile = tiles[0, t]
            live = tile >= 0
            block = jnp.clip(tile - first, 0, blocks - 1)
            ids = enc_edges[t]
            target = one_hot_cols(jnp.where(live, ids[1:2], -1))
            picked = jnp.concatenate([one_hot_cols(ids[0:1]), target], axis=0)
            table = jnp.concatenate([gcat[block], mcat[...]], axis=0)
            pre = mm_first(picked, table)
            mh, ml = split(silu(pre[:, :hid] + pre[:, hid:]))
            messages.append(jnp.concatenate([mh, ml], axis=1))
            hots.append(target)
        acc[...] += mm(jnp.concatenate(hots, axis=1), jnp.concatenate(messages, axis=0))
        return carry

    half_way = slots // group // 2
    fetch("enc_edges").wait()
    lax.fori_loop(0, half_way, edges, 0)
    weight_pass_on(0)
    lax.fori_loop(half_way, slots // group, edges, 0)
    agg_all[me] = acc[:, :hid] + acc[:, hid:]
    for k in range(1, MP):
        y_copy(5, k, agg_all.at[me], agg_all.at[me]).start()
    weight_finish(0)
    for k in range(1, MP):
        y_copy(5, k, agg_all.at[me], agg_all.at[y_from[k]]).wait_recv()
    agg = jnp.concatenate([agg_all[m] for m in range(MP)], axis=1)
    width = grid_hbm.shape[1]
    mesh_one = held["mesh_latent"][...] + product(agg, enc_out_all[...].reshape(width, width))
    normed = norm_rows(mesh_one, got("block_gain"))
    own_kv = product(normed, jnp.concatenate([got("key_w"), got("value_w")], axis=1))
    here = core * CHIPS + chip
    kv[here] = own_kv

    def link_copy(chunk, pos, slot, step):
        start, size = CHUNKS[chunk]
        piece = kv.at[pos, pl.ds(start, size)]
        return pltpu.make_async_remote_copy(
            src_ref=piece,
            dst_ref=piece,
            send_sem=link_send,
            recv_sem=link_recv.at[chunk, slot],
            device_id={"nodes": chip_node(*step)},
            device_id_type=MESH,
        )

    def core_copy(ref):
        return pltpu.make_async_remote_copy(
            src_ref=ref,
            dst_ref=ref,
            send_sem=core_send,
            recv_sem=core_recv,
            device_id={"nodes": sibling},
            device_id_type=MESH,
        )

    starts = [(chunk, step) for chunk in range(len(CHUNKS)) for step in onward(chunk, 0, 0)]
    for chunk, step in sorted(starts, key=lambda s: not branching(*s)):
        link_copy(chunk, here, slot_of(chunk, *step), step).start()
    core_copy(kv.at[here]).start()
    weight_start(1)

    def arrive(event):
        _, chunk, dz, dx, slot = event
        pos = core * CHIPS + z_at[-dz] * X + x_at[-dx]
        start, size = CHUNKS[chunk]
        link_copy(chunk, pos, slot, (1, 0)).wait_recv()
        for step in onward(chunk, dz, dx):
            link_copy(
                chunk, pos, slot_of(chunk, dz + step[0], dx + step[1]), step
            ).start()
        core_copy(kv.at[pos, pl.ds(start, size)]).start()

    nh, nl = split(normed)
    uh, ul = split(got("up_w"))
    hidden = silu(mm3(nh, nl, uh, ul))
    queue = arrivals()
    near = [e for e in queue if e[0][0] == 1]
    rest = [e for e in queue if e[0][0] > 1]
    assert gdec.shape[0] == 4 * BLOCK
    for event in near:
        arrive(event)
    hh, hl = split(hidden)
    dh, dl = split(got("down_w"))
    partial[...] = mm3(hh, hl, dh, dl)
    share = BLOCK // MP

    def share_of(m):
        return pl.ds(pl.multiple_of(m * share, share), share)

    for k in range(1, MP):
        y_copy(6, k, partial.at[share_of(y_at[k])], parts.at[me]).start()
    for item in (2, 3, 4):
        weight_start(item)
    weight_pass_on(1)
    rest_count = len(rest)
    third = rest_count // 4
    for event in rest[:third]:
        arrive(event)
    weight_finish(1)
    gh, gl = split(jnp.concatenate([dec_grid_all[m] for m in range(MP)], axis=1))

    def grid_decode(b):
        block = jnp.clip(order[0, me * MP + b], 0, blocks - 1)
        xh, xl = split(grid_ref[block])
        high, low = split(mm3(xh, xl, gh, gl))
        gdec[b * BLOCK : (b + 1) * BLOCK, :width] = high
        gdec[b * BLOCK : (b + 1) * BLOCK, width:] = low

    grid_decode(0)
    for k in range(1, MP):
        y_copy(6, k, partial.at[share_of(y_at[k])], parts.at[y_from[k]]).wait_recv()
    summed[share_of(me), :] = partial[share_of(me), :] + (
        parts[y_from[1]] + parts[y_from[2]] + parts[y_from[3]]
    )
    for k in range(1, MP):
        y_copy(7, k, summed.at[share_of(me)], summed.at[share_of(me)]).start()
    queries = product(normed, got("query_w")) * (1.0 / math.sqrt(HEAD_DIM))
    for event in rest[third : 2 * third]:
        arrive(event)
    grid_decode(1)
    weight_pass_on(2)
    for event in rest[2 * third : 3 * third]:
        arrive(event)
    grid_decode(2)
    weight_pass_on(3)
    for event in rest[3 * third :]:
        arrive(event)
    weight_pass_on(4)
    grid_decode(3)
    for k in range(1, MP):
        y_copy(7, k, summed.at[share_of(me)], summed.at[share_of(y_from[k])]).wait_recv()
    mesh_mid = mesh_one + summed[...]
    for item, whole in ((2, out_cat), (3, dec_cat)):
        weight_finish(item)
        if item == 2:
            high, low = split(out_all[...].reshape(width, width))
        else:
            high, low = split(jnp.concatenate([dec_mesh_all[m] for m in range(MP)], axis=1))
        whole[:, :width] = high
        whole[:, width:] = low
    core_copy(kv.at[pl.ds((1 - core) * CHIPS, CHIPS)]).wait_recv()

    count = lists.shape[0]
    top = jnp.full((BLOCK, 1), -jnp.inf, F32)
    spots = []
    for j in range(count):
        block = lists[j, node]
        spot = jnp.bitwise_and(block, 1) * CHIPS + jnp.right_shift(block, 1)
        spots.append(spot)
        logit = lax.dot_general(
            queries,
            kv[spot][:, :HEAD_DIM],
            (((1,), (1,)), ((), ())),
            precision=FULL,
            preferred_element_type=F32,
        )
        scores[:, j * BLOCK : (j + 1) * BLOCK] = logit
        top = jnp.maximum(top, jnp.max(logit, axis=-1, keepdims=True))
    weight = jnp.exp(scores[...] - top)
    total = jnp.sum(weight, axis=-1, keepdims=True)
    values = jnp.concatenate([kv[spot][:, HEAD_DIM:] for spot in spots], axis=0)
    wh, wl = split(weight)
    vh, vl = split(values)
    att_all[me] = mm3(wh, wl, vh, vl) / total
    for k in range(1, MP):
        y_copy(8, k, att_all.at[me], att_all.at[me]).start()
    for k in range(1, MP):
        y_copy(8, k, att_all.at[me], att_all.at[y_from[k]]).wait_recv()
    attended = jnp.concatenate([att_all[m] for m in range(MP)], axis=1)
    mesh_two = mesh_mid + mm3(*split(attended), out_cat[:, :width], out_cat[:, width:])
    normed_two = norm_rows(mesh_two, got("dec_gain"))
    th, tl = split(normed_two)
    part_width = width // 2

    def side_copy(way, part, slot, target):
        columns = pl.ds(part * part_width, part_width)
        return pltpu.make_async_remote_copy(
            src_ref=beside.at[1, :, columns],
            dst_ref=beside.at[slot, :, columns],
            send_sem=side_send.at[way, part],
            recv_sem=side_recv.at[way, part],
            device_id={"nodes": target},
            device_id_type=MESH,
        )

    for part in range(2):
        low, high = part * part_width, (part + 1) * part_width
        beside[1, :, low:high] = mm3(
            th, tl, dec_cat[:, low:high], dec_cat[:, width + low : width + high]
        )
        side_copy(0, part, 0, after).start()
        side_copy(1, part, 2, before).start()
    weight_finish(4)
    core_copy(kv.at[pl.ds(core * CHIPS, CHIPS)]).wait_send()
    link_copy_all = pltpu.make_async_remote_copy(
        src_ref=kv.at[pl.ds(0, CHIPS - 1)],
        dst_ref=kv.at[pl.ds(0, CHIPS - 1)],
        send_sem=link_send,
        recv_sem=link_recv.at[0, 0],
        device_id={"nodes": sibling},
        device_id_type=MESH,
    )
    link_copy_all.wait_send()
    for item, ref in ((5, agg_all.at[me]), (8, att_all.at[me])):
        for k in range(1, MP):
            y_copy(item, k, ref, ref).wait_send()
    for item in (6, 7):
        for k in range(1, MP):
            ref = summed.at[share_of(me)]
            y_copy(item, k, ref, ref).wait_send()
    for part in range(2):
        side_copy(0, part, 0, after).wait()
        side_copy(1, part, 2, before).wait()


def mesh_part(tiles, lists, order, grid_latent, arrays):
    rows, width = grid_latent.shape
    nodes = arrays["mesh_latent"].shape[0]
    hid = arrays["enc_grid_w"].shape[1]
    vmem = pl.BlockSpec(memory_space=pltpu.VMEM)
    smem = pl.BlockSpec(memory_space=pltpu.SMEM)
    hbm = pl.BlockSpec(memory_space=pltpu.HBM)
    dma = pltpu.SemaphoreType.DMA
    listed = lists.shape[0]
    operands = [arrays[name] for name in FETCHED]
    return pl.pallas_call(
        mesh_kernel,
        in_specs=[smem, smem, smem, hbm] + [hbm] * len(operands),
        out_specs=[vmem] * 3,
        out_shape=[
            jax.ShapeDtypeStruct((3, nodes, width), F32),
            jax.ShapeDtypeStruct((rows // MP, 2 * width), BF16),
            jax.ShapeDtypeStruct((MP, hid, width), F32),
        ],
        scratch_shapes=[pltpu.VMEM(array.shape, array.dtype) for array in operands]
        + [
            pltpu.VMEM((rows // BLOCK, BLOCK, width), F32),
            pltpu.VMEM((width, 2 * hid), BF16),
            pltpu.VMEM((rows // BLOCK, BLOCK, 2 * hid), BF16),
            pltpu.VMEM((nodes, 2 * hid), BF16),
            pltpu.VMEM((nodes, 2 * hid), F32),
            pltpu.VMEM((MP, nodes, hid), F32),
            pltpu.VMEM((MP, hid, width), F32),
            pltpu.VMEM((MP, hid, width), F32),
            pltpu.VMEM((MP, width, hid), F32),
            pltpu.VMEM((MP, width, hid), F32),
            pltpu.VMEM((2 * CHIPS, nodes, 2 * HEAD_DIM), F32),
            pltpu.VMEM((nodes, width), F32),
            pltpu.VMEM((MP, nodes // MP, width), F32),
            pltpu.VMEM((nodes, width), F32),
            pltpu.VMEM((MP, nodes, HEAD_DIM), F32),
            pltpu.VMEM((nodes, listed * BLOCK), F32),
            pltpu.VMEM((width, 2 * width), BF16),
            pltpu.VMEM((width, 2 * width), BF16),
            dma((len(operands),)),
            dma((rows // 256,)),
            dma((9, MP - 1)),
            dma((9, MP - 1)),
            dma((5, MP - 1)),
            dma((5, MP - 1)),
            dma(()),
            dma((len(CHUNKS), CHIPS)),
            dma(()),
            dma(()),
            dma((2, 2)),
            dma((2, 2)),
        ],
        compiler_params=pltpu.CompilerParams(
            collective_id=0, has_side_effects=True, vmem_limit_bytes=62 << 20
        ),
        name="mesh_part",
    )(tiles, lists, order, grid_latent, *operands)


def assign_kernel(tiles_ref, order_ref):
    blocks = MP * MP
    width = tiles_ref.shape[1]
    first = lax.axis_index("nodes") * blocks
    ids = tiles_ref[1:2, :] - first
    block = lax.broadcasted_iota(jnp.int32, (blocks, width), 0)
    tally = jnp.sum(jnp.where(ids == block, 1.0, 0.0), axis=1, keepdims=True)
    wide = jnp.broadcast_to(tally, (blocks, BLOCK))
    across = jnp.concatenate([wide] * (BLOCK // blocks), axis=0).T[:blocks, :blocks]
    down = wide[:, :blocks]
    i = lax.broadcasted_iota(jnp.int32, (blocks, blocks), 0)
    j = lax.broadcasted_iota(jnp.int32, (blocks, blocks), 1)
    ahead = jnp.logical_or(across > down, jnp.logical_and(across == down, j < i))
    rank = jnp.sum(jnp.where(ahead, 1.0, 0.0), axis=1, keepdims=True).astype(jnp.int32)
    device, turn = j // MP, lax.rem(j, MP)
    dealt = jnp.where(lax.rem(turn, 2) == 0, device, MP - 1 - device) + turn * MP
    chosen = jnp.where(rank == dealt, i.astype(F32), 0.0)
    order_ref[...] = jnp.sum(chosen, axis=0, keepdims=True).astype(jnp.int32)


def assign(dec_tiles):
    vmem = pl.BlockSpec(memory_space=pltpu.VMEM)
    return pl.pallas_call(
        assign_kernel,
        in_specs=[vmem],
        out_specs=vmem,
        out_shape=jax.ShapeDtypeStruct((1, MP * MP), jnp.int32),
        name="assign",
    )(dec_tiles)


def exchange_kernel(agg_hbm, wo_hbm, out_ref, agg, wo_ref, rows_ref, send, recv, fetch):
    me = lax.axis_index("mp")
    share, hid = agg_hbm.shape
    width = wo_hbm.shape[2] // MP
    blocks = share // BLOCK
    y_at = [lax.rem(me + k, MP) for k in range(MP)]
    y_from = [lax.rem(me + MP - k, MP) for k in range(MP)]

    def get(b):
        here = pl.ds(b * BLOCK, BLOCK)
        return pltpu.make_async_copy(agg_hbm.at[here], agg.at[here], fetch.at[b])

    get_wo = pltpu.make_async_copy(wo_hbm, wo_ref, fetch.at[blocks])
    get_wo.start()
    for b in range(blocks):
        get(b).start()
    barrier = pltpu.get_barrier_semaphore()
    for k in range(1, MP):
        pl.semaphore_signal(barrier, inc=1, device_id={"mp": y_at[k]}, device_id_type=MESH)
    get_wo.wait()
    wh, wl = split(wo_ref[...].reshape(hid, MP * width))

    def copy(b, k, at):
        return pltpu.make_async_remote_copy(
            src_ref=rows_ref.at[y_at[k], pl.ds(b * BLOCK, BLOCK)],
            dst_ref=out_ref.at[at * blocks + b],
            send_sem=send.at[b, k - 1],
            recv_sem=recv.at[b, k - 1],
            device_id={"mp": y_at[k]},
            device_id_type=MESH,
        )

    for b in range(blocks):
        get(b).wait()
        here = slice(b * BLOCK, (b + 1) * BLOCK)
        ah, al = split(agg[here, :])
        done = mm3(ah, al, wh, wl)
        for m in range(MP):
            rows_ref[m, here, :] = done[:, m * width : (m + 1) * width]
        if b == 0:
            pl.semaphore_wait(barrier, MP - 1)
        for k in (2, 1, 3):
            copy(b, k, me).start()
        out_ref[me * blocks + b] = rows_ref[me, here, :]
    for b in range(blocks):
        for k in range(1, MP):
            copy(b, k, y_from[k]).wait_recv()
            copy(b, k, me).wait_send()


def exchange(agg, dec_out_w):
    dma = pltpu.SemaphoreType.DMA
    vmem = pl.BlockSpec(memory_space=pltpu.VMEM)
    hbm = pl.BlockSpec(memory_space=pltpu.HBM)
    share, hid = agg.shape
    width = dec_out_w.shape[2] // MP
    blocks = share // BLOCK
    return pl.pallas_call(
        exchange_kernel,
        in_specs=[hbm, hbm],
        out_specs=vmem,
        out_shape=jax.ShapeDtypeStruct((MP * blocks, BLOCK, width), F32),
        scratch_shapes=[
            pltpu.VMEM((share, hid), F32),
            pltpu.VMEM(dec_out_w.shape, F32),
            pltpu.VMEM((MP, share, width), F32),
            dma((blocks, MP - 1)),
            dma((blocks, MP - 1)),
            dma((blocks + 1,)),
        ],
        compiler_params=pltpu.CompilerParams(
            collective_id=1, has_side_effects=True, vmem_limit_bytes=62 << 20
        ),
        name="exchange",
    )(agg, dec_out_w)


def finish_kernel(order, grid_hbm, rows_hbm, out_hbm, held, rows_ref, sums, sems, row_sems, out_sems):
    blocks, _, width = rows_hbm.shape
    columns = pl.ds(pl.multiple_of(lax.axis_index("mp") * width, width), width)

    def place(p):
        return pl.ds(pl.multiple_of(order[0, p] * BLOCK, BLOCK), BLOCK)

    def get(p):
        return pltpu.make_async_copy(grid_hbm.at[place(p), columns], held.at[p], sems.at[p])

    def put(p):
        return pltpu.make_async_copy(sums.at[p], out_hbm.at[place(p)], out_sems.at[p])

    def get_rows(p):
        return pltpu.make_async_copy(rows_hbm.at[p], rows_ref.at[p], row_sems.at[p])

    for p in range(blocks):
        get_rows(p).start()
        get(p).start()
    for p in range(blocks):
        get_rows(p).wait()
        get(p).wait()
        sums[p] = held[p] + rows_ref[p]
        put(p).start()
    for p in range(blocks):
        put(p).wait()


def finish(order, grid_latent, rows):
    blocks, _, width = rows.shape
    hbm = pl.BlockSpec(memory_space=pltpu.HBM)
    dma = pltpu.SemaphoreType.DMA
    return pl.pallas_call(
        finish_kernel,
        in_specs=[pl.BlockSpec(memory_space=pltpu.SMEM), hbm, hbm],
        out_specs=hbm,
        out_shape=jax.ShapeDtypeStruct((blocks * BLOCK, width), F32),
        scratch_shapes=[
            pltpu.VMEM(rows.shape, F32),
            pltpu.VMEM(rows.shape, F32),
            pltpu.VMEM(rows.shape, F32),
            dma((blocks,)),
            dma((blocks,)),
            dma((blocks,)),
        ],
        compiler_params=pltpu.CompilerParams(vmem_limit_bytes=62 << 20),
        name="finish",
    )(order, grid_latent, rows)


def decoder_kernel(
    tiles, order, edges_hbm, gcat_hbm, mesh_hbm, agg, edges_ref, gcat, mesh_ref, mcat, todo, sems
):
    rows, hid = agg.shape
    width = mesh_hbm.shape[2]
    blocks = rows // BLOCK
    node = lax.axis_index("nodes")
    nodes = lax.axis_size("nodes")
    me = lax.axis_index("mp")
    first = node * MP * blocks
    group = 2
    fetch_mesh = pltpu.make_async_copy(mesh_hbm, mesh_ref, sems.at[0])
    fetch_mesh.start()
    fetch_edges = pltpu.make_async_copy(edges_hbm, edges_ref, sems.at[1])
    fetch_edges.start()
    fetch_gcat = pltpu.make_async_copy(gcat_hbm, gcat, sems.at[2])
    fetch_gcat.start()
    agg[...] = jnp.zeros_like(agg)
    mine = [order[0, me * blocks + s] for s in range(blocks)]
    fetch_mesh.wait()
    high, low = split(mesh_ref[...].reshape(-1, width))
    mcat[:, :hid] = high
    mcat[:, hid:] = low
    fetch_edges.wait()
    fetch_gcat.wait()

    def pick(t, found):
        block = tiles[1, t] - first
        spot = jnp.int32(-1)
        for s in range(blocks):
            spot = jnp.where(block == mine[s], s, spot)
        todo[0, found] = t
        todo[1, found] = spot
        return found + jnp.where(spot >= 0, 1, 0)

    found = lax.fori_loop(0, edges_ref.shape[0], pick, jnp.int32(0))
    for k in range(group):
        todo[0, found + k] = 0
        todo[1, found + k] = -1

    def body(i, carry):
        for k in range(group):
            t, spot = todo[0, i * group + k], todo[1, i * group + k]
            live = spot >= 0
            beside = lax.rem(tiles[0, t] - (node - 1) + nodes, nodes)
            ids = edges_ref[t]
            hot = one_hot_cols(jnp.where(live, ids[1:2], -1))
            picked = jnp.concatenate([one_hot_cols(ids[0:1]), hot], axis=0)
            here = pl.ds(pl.multiple_of(jnp.maximum(spot, 0) * BLOCK, BLOCK), BLOCK)
            there = pl.ds(pl.multiple_of(beside * BLOCK, BLOCK), BLOCK)
            table = jnp.concatenate([mcat[there, :], gcat[here, :]], axis=0)
            pre = mm_first(picked, table)
            mh, ml = split(silu(pre[:, :hid] + pre[:, hid:]))
            agg[here, :] += mm(hot, mh) + mm(hot, ml)
        return carry

    lax.fori_loop(0, (found + group - 1) // group, body, 0)


def decoder(gdec, mesh_beside, dec_tiles, dec_edges, order):
    share, hid = gdec.shape[0], gdec.shape[1] // 2
    smem = pl.BlockSpec(memory_space=pltpu.SMEM)
    hbm = pl.BlockSpec(memory_space=pltpu.HBM)
    return pl.pallas_call(
        decoder_kernel,
        in_specs=[smem, smem, hbm, hbm, hbm],
        out_specs=pl.BlockSpec(memory_space=pltpu.VMEM),
        out_shape=jax.ShapeDtypeStruct((share, hid), F32),
        scratch_shapes=[
            pltpu.VMEM(dec_edges.shape, jnp.int32),
            pltpu.VMEM(gdec.shape, BF16),
            pltpu.VMEM(mesh_beside.shape, F32),
            pltpu.VMEM((3 * BLOCK, 2 * hid), BF16),
            pltpu.SMEM((2, dec_edges.shape[0] + 8), jnp.int32),
            pltpu.SemaphoreType.DMA((3,)),
        ],
        compiler_params=pltpu.CompilerParams(vmem_limit_bytes=62 << 20),
        name="decoder",
    )(dec_tiles, order, dec_edges, gdec, mesh_beside)


def per_device(
    grid_latent,
    mesh_latent,
    enc_grid_w,
    enc_mesh_w,
    enc_out_w,
    block_gain,
    query_w,
    key_w,
    value_w,
    out_w,
    up_w,
    down_w,
    dec_gain,
    dec_grid_w,
    dec_mesh_w,
    dec_out_w,
    neighbor_blocks,
    enc_tiles,
    enc_edges,
    dec_tiles,
    dec_edges,
):
    arrays = dict(
        enc_grid_w=enc_grid_w,
        mesh_latent=mesh_latent,
        enc_mesh_w=enc_mesh_w,
        enc_edges=enc_edges,
        enc_out_w=enc_out_w,
        block_gain=block_gain[None],
        query_w=query_w,
        key_w=key_w,
        value_w=value_w,
        out_w=out_w,
        up_w=up_w,
        down_w=down_w,
        dec_gain=dec_gain[None],
        dec_grid_w=dec_grid_w,
        dec_mesh_w=dec_mesh_w,
        dec_out_w=dec_out_w,
    )
    order = assign(dec_tiles.T)
    beside, gdec, dec_out_all = mesh_part(
        enc_tiles.T, neighbor_blocks.T, order, grid_latent, arrays
    )
    agg = decoder(gdec, beside, dec_tiles.T, dec_edges, order)
    return finish(order, grid_latent, exchange(agg, dec_out_all))


def solution(mesh):
    in_specs = (
        P("nodes", None),
        P("nodes", None),
        P(None, "mp"),
        P(None, "mp"),
        P("mp", None),
        P(),
        P(None, "mp"),
        P(None, "mp"),
        P(None, "mp"),
        P("mp", None),
        P(None, "mp"),
        P("mp", None),
        P(),
        P(None, "mp"),
        P(None, "mp"),
        P("mp", None),
        P(),
        P("nodes", None),
        P("nodes", None, None),
        P("nodes", None),
        P("nodes", None, None),
    )
    out_specs = P("nodes", "mp")
    return jax.shard_map(
        per_device, mesh=mesh, in_specs=in_specs, out_specs=out_specs, check_vma=False
    )
```
